32 devices in a mesh: row: 4 (over x, core), col: 8 (over z, y).
Axes of the slice: x: 2, y: 2, z: 4, core: 2. Of those that a mesh axis runs over, the one named last changes fastest.
Arguments:
- factors_u: bfloat16 [128, 1024, 128], P('row', 'col'), may hold values from -6 to 6
- covariates: bfloat16 [128, 1024, 512], P('row', 'col'), may hold values from -6 to 6
- link_beta: float32 [512, 128], replicated, may hold values from -0.25 to 0.25
- factors_v: float32 [4096, 128], P(('row', 'col')), may hold values from -0.5 to 0.5
- obs_values: bfloat16 [32, 128, 128, 128], P(('row', 'col')), may hold values from -6 to 6
- obs_blocks: int32 [32, 128], P(('row', 'col')), may hold values from 0 to 1023, as said below
- obs_count: int32 [32], P(('row', 'col')), may hold values from 1 to 128, as said below
- noise_u: bfloat16 [128, 1024, 128], P('row', 'col'), may hold values from -5 to 5
- noise_v: float32 [4096, 128], P(('row', 'col')), may hold values from -5 to 5
- noise_beta: float32 [512, 128], replicated, may hold values from -5 to 5
Outputs:
- u_next: bfloat16 [128, 1024, 128], P('row', 'col')
- v_next: float32 [4096, 128], P(('row', 'col'))
- beta_next: float32 [512, 128], replicated
The draws below stay inside these ranges and needn't reach their ends.
Inputs may be any that keep to these rules, and one draw needn't show every extreme that they name: `obs_blocks`: A device's entries are distinct numbers pb * 32 + db with pb below 32. `obs_count`: some device's count is 128 in every draw.
All inputs are finite; a program needn't handle non-finite values.
Results may differ from the reference program's by a relative error of at most 0.0095.
Values may be sent and summed in bfloat16 or wider, within the bound.
A program may use at most 64 MiB of HBM per device.

```python
import math
import jax
import jax.numpy as jnp
from jax import lax

K = 128
NCOV = 512
BLK = 128
DAYS = 4096
TR = 32
NB_CAP = 128
PIX_R = 128
PIX_C = 1024
N_ROW = 4
N_COL = 8


def place_value(order, wanted, position):
    found = jnp.argmax(order == wanted)
    previous = order[position]
    order = order.at[found].set(previous)
    return order.at[position].set(wanted)


def draw_obs_blocks(key, part):
    device_count = N_ROW * N_COL
    total = TR * (DAYS // BLK)
    keys = jax.random.split(jax.random.fold_in(key, 11), device_count)
    chosen = jax.random.randint(jax.random.fold_in(key, 37), (), 0, device_count)

    def single(one_key, device):
        order = jax.random.permutation(one_key, total).astype(jnp.int32)
        forced = place_value(order, jnp.int32(total - 1), 0)
        forced = place_value(forced, jnp.int32(0), 1)
        order = jnp.where(device == chosen, forced, order)
        return order[:NB_CAP]
    return jax.vmap(single)(keys, jnp.arange(device_count)).astype(jnp.int32)


def draw_obs_count(key, part):
    device_count = N_ROW * N_COL
    first_key, second_key = jax.random.split(jax.random.fold_in(key, 23))
    shifts = jax.random.randint(first_key, (device_count,), 0, 4)
    counts = jnp.right_shift(jnp.full((device_count,), NB_CAP, jnp.int32), shifts)
    busiest = jax.random.randint(second_key, (), 0, device_count)
    counts = jnp.where(jnp.arange(device_count) == busiest, NB_CAP, counts)
    return counts.astype(jnp.int32)


def steps_of(stream_key, dims, pieces, smallest, high):
    loudness, own = 1.0, jax.random.fold_in(stream_key, 6)
    for axis_at, shards_of in pieces:
        draws = jnp.exp(jax.random.uniform(jax.random.fold_in(own, axis_at), (shards_of,), jnp.float32, smallest / len(pieces), high / len(pieces)))
        loudness = loudness * jnp.repeat(draws, dims[axis_at] // shards_of).reshape([-1 if axis == axis_at else 1 for axis in range(len(dims))])
    return loudness


def scatter_about(rng, shape, scale, limit, cuts=(), dtype=jnp.bfloat16):
    array = scale * jax.random.normal(rng, shape, jnp.float32)
    if cuts:
        array = array * steps_of(rng, shape, cuts, -0.22, 0.18)
    return jnp.clip(array, -limit, limit).astype(dtype)


def setup_inputs(seed: int = 0) -> dict:
    streams_of = jax.random.split(jax.random.key(seed), 11)
    factors_u = scatter_about(streams_of[0], (PIX_R, PIX_C, K), 1.0, 6.0, ((0, 4), (1, 8)))
    covariates = scatter_about(streams_of[1], (PIX_R, PIX_C, NCOV), 1.0, 6.0, ((0, 4), (1, 8)))
    link_beta = scatter_about(streams_of[2], (NCOV, K), NCOV ** -0.5, 0.25, (), jnp.float32)
    factors_v = scatter_about(streams_of[3], (DAYS, K), K ** -0.5, 0.5, ((0, 32),), jnp.float32)
    obs_values = scatter_about(streams_of[4], (N_ROW * N_COL, NB_CAP, BLK, BLK), 1.0, 6.0, ((0, 32),))
    obs_blocks = draw_obs_blocks(jax.random.fold_in(streams_of[10], 71), 0)
    obs_count = draw_obs_count(jax.random.fold_in(streams_of[10], 71), 0)
    noise_u = scatter_about(streams_of[7], (PIX_R, PIX_C, K), 1.0, 5.0, ((0, 4), (1, 8)))
    noise_v = scatter_about(streams_of[8], (DAYS, K), 1.0, 5.0, ((0, 32),), jnp.float32)
    noise_beta = scatter_about(streams_of[9], (NCOV, K), 1.0, 5.0, (), jnp.float32)
    return dict(factors_u=factors_u, covariates=covariates, link_beta=link_beta, factors_v=factors_v, obs_values=obs_values, obs_blocks=obs_blocks, obs_count=obs_count, noise_u=noise_u, noise_v=noise_v, noise_beta=noise_beta)


edge_weight = 0.5
ridge_weight = 0.1
step_pixel = 0.2

def reference(factors_u, covariates, link_beta, factors_v, obs_values, obs_blocks, obs_count, noise_u, noise_v, noise_beta):
    device_count = N_ROW * N_COL
    day_blocks = DAYS // BLK
    beta_bf = link_beta.astype(jnp.bfloat16)
    covar_rows = covariates.reshape(-1, NCOV)
    mean_field = jnp.dot(covar_rows, beta_bf, preferred_element_type=jnp.float32).reshape(PIX_R, PIX_C, K)
    resid_field = factors_u.astype(jnp.float32) - mean_field
    padded = jnp.pad(resid_field, ((1, 1), (1, 1), (0, 0)))
    laplace = 4.0 * resid_field - (padded[2:, 1:-1] + padded[:-2, 1:-1] + padded[1:-1, 2:] + padded[1:-1, :-2])
    prior_pull = edge_weight * laplace + ridge_weight * resid_field
    prior_bf = prior_pull.astype(jnp.bfloat16)
    link_grad = lax.dot_general(covar_rows, prior_bf.reshape(-1, K), (((0,), (0,)), ((), ())), preferred_element_type=jnp.float32)
    days_bf = factors_v.astype(jnp.bfloat16).reshape(day_blocks, BLK, K)
    tiles = factors_u.reshape(N_ROW, TR, N_COL, BLK, K).transpose(0, 2, 1, 3, 4).reshape(device_count, TR, BLK, K)

    def per_device(carried, inputs):
        tile_u, values, blocks, live_count = inputs
        pixel_ids = (blocks // day_blocks).astype(jnp.int32)
        day_ids = (blocks % day_blocks).astype(jnp.int32)
        u_rows = tile_u[pixel_ids].astype(jnp.float32)
        v_rows = days_bf[day_ids].astype(jnp.float32)
        predicted = jnp.einsum('pbk,pdk->pbd', u_rows, v_rows)
        is_live = jnp.arange(NB_CAP) < live_count
        residual = jnp.where(is_live[:, None, None], values.astype(jnp.float32) - predicted, 0.0).astype(jnp.bfloat16)
        res_wide = residual.astype(jnp.float32)
        grad_rows = jnp.einsum('pbd,pdk->pbk', res_wide, v_rows)
        day_terms = jnp.einsum('pbd,pbk->pdk', res_wide, u_rows)
        data_tile = jax.ops.segment_sum(grad_rows, pixel_ids, num_segments=TR)
        carried = carried + jax.ops.segment_sum(day_terms, day_ids, num_segments=day_blocks)
        return (carried, data_tile)
    data_v, data_tiles = lax.scan(per_device, jnp.zeros((day_blocks, BLK, K), jnp.float32), (tiles, obs_values, obs_blocks, obs_count))
    data_u = data_tiles.reshape(N_ROW, N_COL, TR, BLK, K).transpose(0, 2, 1, 3, 4).reshape(PIX_R, PIX_C, K)
    u_next = (factors_u.astype(jnp.float32) + 0.5 * step_pixel * (data_u - prior_pull) + math.sqrt(step_pixel) * noise_u.astype(jnp.float32)).astype(jnp.bfloat16)
    step_day = 0.25 / math.sqrt(device_count * NB_CAP * BLK / day_blocks)
    v_next = factors_v + 0.5 * step_day * (data_v.reshape(DAYS, K) - factors_v) + math.sqrt(step_day) * noise_v
    step_link = 0.25 / math.sqrt(device_count * TR * BLK)
    beta_next = link_beta + 0.5 * step_link * (link_grad - link_beta) + math.sqrt(step_link) * noise_beta
    return (u_next, v_next, beta_next)
```

```python
import functools
import math

import jax
import jax.numpy as jnp
from jax import lax
from jax.experimental import pallas as pl
from jax.experimental.pallas import tpu as pltpu
from jax.sharding import PartitionSpec as P

edge_weight = 0.5
ridge_weight = 0.1
step_pixel = 0.2
MESH = pl.DeviceIdType.MESH
F32 = jnp.float32
BF16 = jnp.bfloat16
VMEM = pl.BlockSpec(memory_space=pltpu.VMEM)
ANY = pl.BlockSpec(memory_space=pl.ANY)
LIMIT = 48 * 1024 * 1024


class Place:
    def __init__(self, rows, cols):
        self.rows, self.cols = rows, cols
        self.nr, self.nc = rows // 2, cols // 2
        self.r, self.c = lax.axis_index("row"), lax.axis_index("col")
        self.r1, self.r0 = self.r // 2, lax.rem(self.r, 2)
        self.c1, self.c0 = self.c // 2, lax.rem(self.c, 2)
        self.core = (self.r1 * 2 + (1 - self.r0), self.c)
        self.side = (self.r, self.c1 * 2 + (1 - self.c0))

    def r1_at(self, k):
        return lax.rem(self.r1 + k, self.nr)

    def c1_at(self, k):
        return lax.rem(self.c1 + k, self.nc)

    def x_peer(self, k):
        return (self.r1_at(k) * 2 + self.r0, self.c)

    def z_peer(self, k):
        return (self.r, self.c1_at(k) * 2 + self.c0)

    def partners(self):
        return (
            [self.core, self.side]
            + [self.x_peer(k) for k in range(1, self.nr)]
            + [self.z_peer(k) for k in range(1, self.nc)]
        )


def greet(partners):
    barrier = pltpu.get_barrier_semaphore()
    for partner in partners:
        pl.semaphore_signal(barrier, inc=1, device_id=partner, device_id_type=MESH)
    pl.semaphore_wait(barrier, len(partners))


def send(src, dst, send_sem, recv_sem, device):
    copy = pltpu.make_async_remote_copy(
        src_ref=src, dst_ref=dst, send_sem=send_sem, recv_sem=recv_sem,
        device_id=device, device_id_type=MESH,
    )
    copy.start()
    return copy


def field_kernel(
    rows, cols, fv_ref, beta_ref, cov_hbm, u_hbm, nz_hbm,
    days, base_ref, link_ref,
    cov, u, nz, beta, rp, edge_send, edge_recv, link_acc,
    load_sem, day_send, day_recv, halo_send, halo_recv,
):
    at = Place(rows, cols)
    nr, nc = at.nr, at.nc
    tile, block = u.shape[0], u.shape[1]
    parts = 4
    per = tile // parts
    loads = []
    for k in range(parts):
        loads.append(pltpu.make_async_copy(cov_hbm.at[pl.ds(k * per, per)], cov.at[pl.ds(k * per, per)], load_sem.at[k]))
    u_load = pltpu.make_async_copy(u_hbm, u, load_sem.at[parts])
    nz_load = pltpu.make_async_copy(nz_hbm, nz, load_sem.at[parts + 1])
    loads[0].start()
    u_load.start()
    for load in loads[1:]:
        load.start()
    nz_load.start()

    days[at.r1, at.r0, at.c1, at.c0] = fv_ref[...].astype(BF16)
    north = (lax.rem(at.r + rows - 1, rows), at.c)
    south = (lax.rem(at.r + 1, rows), at.c)
    west = (at.r, lax.rem(at.c + cols - 1, cols))
    east = (at.r, lax.rem(at.c + 1, cols))
    greet(at.partners() + [north, south, west, east])

    sends = []

    def block_at(b):
        return days.at[b[0], b[1], b[2], b[3]]

    def sem_at(b):
        return day_recv.at[((b[0] * 2 + b[1]) * nc + b[2]) * 2 + b[3]]

    def pass_on(b, partners):
        for partner in partners:
            sends.append(send(block_at(b), block_at(b), day_send.at[len(sends)], sem_at(b), partner))

    def arrive(b):
        pltpu.make_async_remote_copy(
            src_ref=block_at(b), dst_ref=block_at(b), send_sem=day_send.at[0], recv_sem=sem_at(b),
            device_id=at.core, device_id_type=MESH,
        ).wait_recv()

    zs = [at.z_peer(k) for k in range(1, nc)]
    xs = [at.x_peer(k) for k in range(1, nr)]
    own = (at.r1, at.r0, at.c1, at.c0)
    pass_on(own, zs + [at.side] + xs + [at.core])

    beta[...] = beta_ref[...].astype(BF16)

    def resid_rows(i):
        cells = cov[pl.ds(i, per)].reshape(per * block, cov.shape[2])
        mean = jnp.dot(cells, beta[...], preferred_element_type=F32)
        rp[pl.ds(i + 1, per)] = u[pl.ds(i, per)].astype(F32) - mean.reshape(per, block, -1)

    u_load.wait()
    for k in range(parts):
        loads[k].wait()
        resid_rows(k * per)
    edge_send[0] = rp[pl.ds(1, tile), 0, :]
    edge_send[1] = rp[pl.ds(1, tile), block - 1, :]
    halos = [
        send(rp.at[1], rp.at[tile + 1], halo_send.at[0], halo_recv.at[0], north),
        send(rp.at[tile], rp.at[0], halo_send.at[1], halo_recv.at[1], south),
        send(edge_send.at[0], edge_recv.at[1], halo_send.at[2], halo_recv.at[2], west),
        send(edge_send.at[1], edge_recv.at[0], halo_send.at[3], halo_recv.at[3], east),
    ]

    for k in range(1, nc):
        b = (at.r1, at.r0, at.c1_at(nc - k), at.c0)
        arrive(b)
        pass_on(b, [at.side] + xs + [at.core])
    for k in range(nc):
        b = (at.r1, at.r0, at.c1_at(nc - k), 1 - at.c0)
        arrive(b)
        pass_on(b, xs + [at.core])

    nz_load.wait()
    for halo in halos:
        halo.wait()
    for spot, gone in ((0, at.r == 0), (tile + 1, at.r == rows - 1)):
        rp[spot] = jnp.where(gone, 0.0, rp[spot])
    for spot, gone in ((0, at.c == 0), (1, at.c == cols - 1)):
        edge_recv[spot] = jnp.where(gone, 0.0, edge_recv[spot])

    lane_row = lax.broadcasted_iota(jnp.int32, (per, block, u.shape[2]), 1)

    def prior_rows(i):
        mid = rp[pl.ds(i + 1, per)]
        around = rp[pl.ds(i, per)] + rp[pl.ds(i + 2, per)]
        left = jnp.where(lane_row == 0, edge_recv[0, pl.ds(i, per)][:, None, :], pltpu.roll(mid, 1, 1))
        right = jnp.where(
            lane_row == block - 1, edge_recv[1, pl.ds(i, per)][:, None, :], pltpu.roll(mid, block - 1, 1)
        )
        laplace = 4.0 * mid - (around + right + left)
        prior = edge_weight * laplace + ridge_weight * mid
        base_ref[pl.ds(i, per)] = (
            u[pl.ds(i, per)].astype(F32)
            - 0.5 * step_pixel * prior
            + math.sqrt(step_pixel) * nz[pl.ds(i, per)].astype(F32)
        )
        return lax.dot_general(
            prior.astype(BF16).reshape(per * block, -1),
            cov[pl.ds(i, per)].reshape(per * block, cov.shape[2]),
            (((0,), (0,)), ((), ())),
            preferred_element_type=F32,
        )

    for k in range(parts):
        if k == 0:
            link_acc[...] = prior_rows(0)
        else:
            link_acc[...] += prior_rows(k * per)

    for j in range(1, nr):
        for k in range(nc):
            for c0 in (at.c0, 1 - at.c0):
                b = (at.r1_at(nr - j), at.r0, at.c1_at(nc - k), c0)
                arrive(b)
                pass_on(b, [at.core])
    link_ref[...] = link_acc[...].T
    for j in range(nr):
        for k in range(nc):
            for c0 in (at.c0, 1 - at.c0):
                arrive((at.r1_at(nr - j), 1 - at.r0, at.c1_at(nc - k), c0))
    for copy in sends:
        copy.wait_send()


def run_field(rows, cols, factors_v, link_beta, covariates, factors_u, noise_u):
    tile, block, rank = factors_u.shape
    covar = covariates.shape[2]
    per_device = factors_v.shape[0]
    count = rows * cols
    return pl.pallas_call(
        functools.partial(field_kernel, rows, cols),
        out_shape=(
            jax.ShapeDtypeStruct((rows // 2, 2, cols // 2, 2, per_device, rank), BF16),
            jax.ShapeDtypeStruct((tile, block, rank), F32),
            jax.ShapeDtypeStruct((covar, rank), F32),
        ),
        in_specs=[VMEM, VMEM, ANY, ANY, ANY],
        out_specs=(VMEM, VMEM, VMEM),
        scratch_shapes=[
            pltpu.VMEM((tile, block, covar), BF16),
            pltpu.VMEM((tile, block, rank), BF16),
            pltpu.VMEM((tile, block, rank), BF16),
            pltpu.VMEM((covar, rank), BF16),
            pltpu.VMEM((tile + 2, block, rank), F32),
            pltpu.VMEM((2, tile, rank), F32),
            pltpu.VMEM((2, tile, rank), F32),
            pltpu.VMEM((rank, covar), F32),
            pltpu.SemaphoreType.DMA((6,)),
            pltpu.SemaphoreType.DMA((count,)),
            pltpu.SemaphoreType.DMA((count,)),
            pltpu.SemaphoreType.DMA((4,)),
            pltpu.SemaphoreType.DMA((4,)),
        ],
        compiler_params=pltpu.CompilerParams(
            collective_id=0, has_side_effects=True, vmem_limit_bytes=LIMIT
        ),
    )(factors_v, link_beta, covariates, factors_u, noise_u)


def slots_kernel(group, blocks_ref, count_ref, obs_ref, u_ref, v_ref, base_ref, next_ref, dv_ref, acc_u, acc_v):
    step = pl.program_id(0)
    day_blocks = v_ref.shape[0]

    @pl.when(step == 0)
    def _():
        acc_u[...] = base_ref[...]
        acc_v[...] = jnp.zeros_like(acc_v)

    live = count_ref[0]
    wide = 4

    def turn(t, carry):
        found = []
        for j in range(wide):
            s = t * wide + j
            slot = step * group + s
            e = blocks_ref[slot]
            pb, db = e // day_blocks, lax.rem(e, day_blocks)
            uu, vv = u_ref[pb], v_ref[db]
            predicted = lax.dot_general(uu, vv, (((1,), (1,)), ((), ())), preferred_element_type=F32)
            residual = jnp.where(slot < live, obs_ref[s].astype(F32) - predicted, 0.0).astype(BF16)
            grad = jnp.dot(residual, vv, preferred_element_type=F32)
            day = lax.dot_general(residual, uu, (((0,), (0,)), ((), ())), preferred_element_type=F32)
            found.append((pb, db, grad, day))
        for pb, db, grad, day in found:
            acc_u[pb] += 0.5 * step_pixel * grad
            acc_v[db] += day
        return carry

    lax.fori_loop(0, group // wide, turn, 0)

    @pl.when(step == pl.num_programs(0) - 1)
    def _():
        next_ref[...] = acc_u[...].astype(BF16)
        dv_ref[...] = acc_v[...].astype(BF16)


def run_slots(blocks, live, obs, factors_u, day_table, base):
    slots, block, _ = obs.shape
    tile, _, rank = factors_u.shape
    day_blocks = day_table.shape[0]
    group = 16
    whole = lambda shape: pl.BlockSpec(shape, lambda i, *_: (0,) * len(shape))
    return pl.pallas_call(
        functools.partial(slots_kernel, group),
        out_shape=(
            jax.ShapeDtypeStruct((tile, block, rank), BF16),
            jax.ShapeDtypeStruct((day_blocks, block, rank), BF16),
        ),
        grid_spec=pltpu.PrefetchScalarGridSpec(
            num_scalar_prefetch=2,
            grid=(slots // group,),
            in_specs=[
                pl.BlockSpec((group, block, block), lambda i, *_: (i, 0, 0)),
                whole(factors_u.shape),
                whole(day_table.shape),
                whole(base.shape),
            ],
            out_specs=(whole((tile, block, rank)), whole((day_blocks, block, rank))),
            scratch_shapes=[
                pltpu.VMEM((tile, block, rank), F32),
                pltpu.VMEM((day_blocks, block, rank), F32),
            ],
        ),
        compiler_params=pltpu.CompilerParams(vmem_limit_bytes=LIMIT),
    )(blocks, live, obs, factors_u, day_table, base)


def sum_kernel(
    rows, cols, step_day, step_link,
    dv, lk, fv_ref, nv_ref, beta_ref, nb_ref,
    v_ref, beta_out,
    got_core, mid_core, got_x, mid_x, got_side, mid_side, got_z,
    lk_core, lm_core, lk_x, lm_x, lk_side, lk_z, total,
    send_sem, recv_sem,
):
    at = Place(rows, cols)
    nr, nc = at.nr, at.nc
    greet(at.partners())
    used = [0]
    pending = []

    def post(src, dst, device):
        k = used[0]
        used[0] += 1
        copy = send(src, dst, send_sem.at[k], recv_sem.at[k], device)
        pending.append(copy)
        return copy

    def settle(copies):
        for copy in copies:
            copy.wait_recv()

    a = [post(dv.at[:, 1 - at.r0], got_core, at.core)]
    b = [post(lk.at[1 - at.r0], lk_core, at.core)]
    settle(a)
    mid_core[...] = (dv[:, at.r0].astype(F32) + got_core[...].astype(F32)).astype(BF16)
    a = [post(mid_core.at[at.r1_at(k)], got_x.at[k - 1], at.x_peer(k)) for k in range(1, nr)]
    settle(b)
    lm_core[...] = lk[at.r0] + lk_core[...]
    b = [post(lm_core.at[at.r1_at(k)], lk_x.at[k - 1], at.x_peer(k)) for k in range(1, nr)]
    settle(a)
    part = mid_core[at.r1].astype(F32)
    for k in range(nr - 1):
        part = part + got_x[k].astype(F32)
    mid_x[...] = part.astype(BF16)
    a = [post(mid_x.at[:, 1 - at.c0], got_side, at.side)]
    settle(b)
    link = lm_core[at.r1]
    for k in range(nr - 1):
        link = link + lk_x[k]
    lm_x[...] = link
    b = [post(lm_x.at[1 - at.c0], lk_side, at.side)]
    settle(a)
    mid_side[...] = (mid_x[:, at.c0].astype(F32) + got_side[...].astype(F32)).astype(BF16)
    a = [post(mid_side.at[at.c1_at(k)], got_z.at[k - 1], at.z_peer(k)) for k in range(1, nc)]
    settle(b)
    lk_z[at.c1] = lm_x[at.c0] + lk_side[...]
    b = [post(lk_z.at[at.c1], lk_z.at[at.c1], at.z_peer(k)) for k in range(1, nc)]
    settle(b)
    link = lk_z[0]
    for k in range(1, nc):
        link = link + lk_z[k]
    total[at.r0, at.r1, at.c0] = link
    b = [post(total.at[at.r0, at.r1, at.c0], total.at[at.r0, at.r1, at.c0], at.side)]
    settle(a)
    part = mid_side[at.c1].astype(F32)
    for k in range(nc - 1):
        part = part + got_z[k].astype(F32)
    old = fv_ref[...]
    v_ref[...] = old + 0.5 * step_day * (part - old) + math.sqrt(step_day) * nv_ref[...]
    settle(b)
    b = [post(total.at[at.r0, at.r1], total.at[at.r0, at.r1], at.x_peer(k)) for k in range(1, nr)]
    settle(b)
    b = [post(total.at[at.r0], total.at[at.r0], at.core)]
    settle(b)
    old = beta_ref[...]
    beta_out[...] = old + 0.5 * step_link * (total[...] - old) + math.sqrt(step_link) * nb_ref[...]
    for copy in pending:
        copy.wait_send()


def run_sum(rows, cols, step_day, step_link, dv, link_part, factors_v, noise_v, link_beta, noise_beta):
    nr, nc = rows // 2, cols // 2
    per_device, rank = factors_v.shape
    covar = link_beta.shape[0]
    piece = covar // (4 * nr)
    lshape = (2, nr, 2, piece, rank)
    sends = 2 * (1 + (nr - 1) + 1 + (nc - 1)) + 1 + (nr - 1) + 1
    v_next, beta_next = pl.pallas_call(
        functools.partial(sum_kernel, rows, cols, step_day, step_link),
        out_shape=(
            jax.ShapeDtypeStruct((per_device, rank), F32),
            jax.ShapeDtypeStruct(lshape, F32),
        ),
        in_specs=[VMEM] * 6,
        out_specs=(VMEM, VMEM),
        scratch_shapes=[
            pltpu.VMEM((nr, nc, 2, per_device, rank), BF16),
            pltpu.VMEM((nr, nc, 2, per_device, rank), BF16),
            pltpu.VMEM((nr - 1, nc, 2, per_device, rank), BF16),
            pltpu.VMEM((nc, 2, per_device, rank), BF16),
            pltpu.VMEM((nc, per_device, rank), BF16),
            pltpu.VMEM((nc, per_device, rank), BF16),
            pltpu.VMEM((nc - 1, per_device, rank), BF16),
            pltpu.VMEM((nr, 2, piece, rank), F32),
            pltpu.VMEM((nr, 2, piece, rank), F32),
            pltpu.VMEM((nr - 1, 2, piece, rank), F32),
            pltpu.VMEM((2, piece, rank), F32),
            pltpu.VMEM((piece, rank), F32),
            pltpu.VMEM((nc, piece, rank), F32),
            pltpu.VMEM(lshape, F32),
            pltpu.SemaphoreType.DMA((sends,)),
            pltpu.SemaphoreType.DMA((sends,)),
        ],
        compiler_params=pltpu.CompilerParams(
            collective_id=1, has_side_effects=True, vmem_limit_bytes=LIMIT
        ),
    )(
        dv.reshape(nr, 2, nc, 2, per_device, rank),
        link_part.reshape(lshape),
        factors_v,
        noise_v,
        link_beta.reshape(lshape),
        noise_beta.reshape(lshape),
    )
    return v_next, beta_next.reshape(covar, rank)


def shards(
    factors_u, covariates, link_beta, factors_v, obs_values, obs_blocks, obs_count,
    noise_u, noise_v, noise_beta,
):
    rows = lax.axis_size("row")
    cols = lax.axis_size("col")
    devices = rows * cols
    tile, block, rank = factors_u.shape
    per_device = factors_v.shape[0]
    days = per_device * devices
    day_blocks = days // block
    slots = obs_blocks.shape[1]
    day_table, base, link_part = run_field(
        rows, cols, factors_v, link_beta, covariates, factors_u, noise_u
    )
    u_next, dv = run_slots(
        obs_blocks[0], obs_count, obs_values[0], factors_u,
        day_table.reshape(day_blocks, block, rank), base,
    )
    step_day = 0.25 / math.sqrt(devices * slots * block / day_blocks)
    step_link = 0.25 / math.sqrt(devices * tile * block)
    v_next, beta_next = run_sum(
        rows, cols, step_day, step_link, dv, link_part, factors_v, noise_v, link_beta, noise_beta
    )
    return (u_next, v_next, beta_next)


def solution(mesh):
    in_specs = (
        P("row", "col", None),
        P("row", "col", None),
        P(),
        P(("row", "col"), None),
        P(("row", "col"), None, None, None),
        P(("row", "col"), None),
        P(("row", "col")),
        P("row", "col", None),
        P(("row", "col"), None),
        P(),
    )
    out_specs = (P("row", "col", None), P(("row", "col"), None), P())
    return jax.shard_map(shards, mesh=mesh, in_specs=in_specs, out_specs=out_specs, check_vma=False)
```

```python
import functools
import math

import jax
import jax.numpy as jnp
from jax import lax
from jax.experimental import pallas as pl
from jax.experimental.pallas import tpu as pltpu
from jax.sharding import PartitionSpec as P

edge_weight = 0.5
ridge_weight = 0.1
step_pixel = 0.2
MESH = pl.DeviceIdType.MESH
F32 = jnp.float32
BF16 = jnp.bfloat16
VMEM = pl.BlockSpec(memory_space=pltpu.VMEM)
ANY = pl.BlockSpec(memory_space=pl.ANY)
LIMIT = 40 * 1024 * 1024


class Place:
    def __init__(self, rows, cols):
        self.rows, self.cols = rows, cols
        self.nr, self.nc = rows // 2, cols // 2
        self.r, self.c = lax.axis_index("row"), lax.axis_index("col")
        self.r1, self.r0 = self.r // 2, lax.rem(self.r, 2)
        self.c1, self.c0 = self.c // 2, lax.rem(self.c, 2)
        self.core = (self.r1 * 2 + (1 - self.r0), self.c)
        self.side = (self.r, self.c1 * 2 + (1 - self.c0))

    def r1_at(self, k):
        return lax.rem(self.r1 + k, self.nr)

    def c1_at(self, k):
        return lax.rem(self.c1 + k, self.nc)

    def x_peer(self, k):
        return (self.r1_at(k) * 2 + self.r0, self.c)

    def z_peer(self, k):
        return (self.r, self.c1_at(k) * 2 + self.c0)

    def partners(self):
        return (
            [self.core, self.side]
            + [self.x_peer(k) for k in range(1, self.nr)]
            + [self.z_peer(k) for k in range(1, self.nc)]
        )


def greet(partners):
    barrier = pltpu.get_barrier_semaphore()
    for partner in partners:
        pl.semaphore_signal(barrier, inc=1, device_id=partner, device_id_type=MESH)
    pl.semaphore_wait(barrier, len(partners))


def send(src, dst, send_sem, recv_sem, device):
    copy = pltpu.make_async_remote_copy(
        src_ref=src, dst_ref=dst, send_sem=send_sem, recv_sem=recv_sem,
        device_id=device, device_id_type=MESH,
    )
    copy.start()
    return copy


def field_kernel(
    rows, cols, blocks_ref, live_ref, fv_ref, beta_ref, cov_hbm, u_hbm, nz_hbm, obs_hbm,
    base_ref, total, grad_ref, term_ref,
    days, cov, u, nz, obs, beta, rp, edge_send, edge_recv, link_acc,
    lk, lk_core, lm_core, lk_x, lm_x, lk_side, lk_z,
    load_sem, day_send, day_recv, halo_send, halo_recv, link_send, link_recv,
):
    at = Place(rows, cols)
    nr, nc = at.nr, at.nc
    tile, block = u.shape[0], u.shape[1]
    parts = 4
    per = tile // parts
    loads = []
    for k in range(parts):
        loads.append(pltpu.make_async_copy(cov_hbm.at[pl.ds(k * per, per)], cov.at[pl.ds(k * per, per)], load_sem.at[k]))
    u_load = pltpu.make_async_copy(u_hbm, u, load_sem.at[parts])
    nz_load = pltpu.make_async_copy(nz_hbm, nz, load_sem.at[parts + 1])
    loads[0].start()
    u_load.start()
    for load in loads[1:]:
        load.start()
    nz_load.start()
    obs_load = pltpu.make_async_copy(obs_hbm, obs, load_sem.at[parts + 2])
    obs_load.start()

    def index_of(b):
        return ((b[0] * 2 + b[1]) * nc + b[2]) * 2 + b[3]

    days[at.r * cols + at.c] = fv_ref[...].astype(BF16)
    north = (lax.rem(at.r + rows - 1, rows), at.c)
    south = (lax.rem(at.r + 1, rows), at.c)
    west = (at.r, lax.rem(at.c + cols - 1, cols))
    east = (at.r, lax.rem(at.c + 1, cols))
    greet(at.partners() + [north, south, west, east])

    sends = []

    def block_at(b):
        return days.at[index_of(b)]

    def sem_at(b):
        return day_recv.at[index_of(b)]

    def pass_on(b, partners):
        for partner in partners:
            sends.append(send(block_at(b), block_at(b), day_send.at[len(sends)], sem_at(b), partner))

    def arrive(b):
        pltpu.make_async_remote_copy(
            src_ref=block_at(b), dst_ref=block_at(b), send_sem=day_send.at[0], recv_sem=sem_at(b),
            device_id=at.core, device_id_type=MESH,
        ).wait_recv()

    zs = [at.z_peer(k) for k in range(1, nc)]
    xs = [at.x_peer(k) for k in range(1, nr)]
    own = (at.r1, at.r0, at.c1, at.c0)
    pass_on(own, zs + [at.side] + xs + [at.core])

    beta[...] = beta_ref[...].astype(BF16)

    def resid_rows(i):
        cells = cov[pl.ds(i, per)].reshape(per * block, cov.shape[2])
        mean = jnp.dot(cells, beta[...], preferred_element_type=F32)
        rp[pl.ds(i + 1, per)] = u[pl.ds(i, per)].astype(F32) - mean.reshape(per, block, -1)

    u_load.wait()
    for k in range(parts):
        loads[k].wait()
        resid_rows(k * per)
    edge_send[0] = rp[pl.ds(1, tile), 0, :]
    edge_send[1] = rp[pl.ds(1, tile), block - 1, :]
    halos = [
        send(rp.at[1], rp.at[tile + 1], halo_send.at[0], halo_recv.at[0], north),
        send(rp.at[tile], rp.at[0], halo_send.at[1], halo_recv.at[1], south),
        send(edge_send.at[0], edge_recv.at[1], halo_send.at[2], halo_recv.at[2], west),
        send(edge_send.at[1], edge_recv.at[0], halo_send.at[3], halo_recv.at[3], east),
    ]

    for k in range(1, nc):
        b = (at.r1, at.r0, at.c1_at(nc - k), at.c0)
        arrive(b)
        pass_on(b, [at.side] + xs + [at.core])
    for k in range(nc):
        b = (at.r1, at.r0, at.c1_at(nc - k), 1 - at.c0)
        arrive(b)
        pass_on(b, xs + [at.core])

    nz_load.wait()
    for halo in halos:
        halo.wait()
    for spot, gone in ((0, at.r == 0), (tile + 1, at.r == rows - 1)):
        rp[spot] = jnp.where(gone, 0.0, rp[spot])
    for spot, gone in ((0, at.c == 0), (1, at.c == cols - 1)):
        edge_recv[spot] = jnp.where(gone, 0.0, edge_recv[spot])

    lane_row = lax.broadcasted_iota(jnp.int32, (per, block, u.shape[2]), 1)

    def prior_rows(i):
        mid = rp[pl.ds(i + 1, per)]
        around = rp[pl.ds(i, per)] + rp[pl.ds(i + 2, per)]
        left = jnp.where(lane_row == 0, edge_recv[0, pl.ds(i, per)][:, None, :], pltpu.roll(mid, 1, 1))
        right = jnp.where(
            lane_row == block - 1, edge_recv[1, pl.ds(i, per)][:, None, :], pltpu.roll(mid, block - 1, 1)
        )
        laplace = 4.0 * mid - (around + right + left)
        prior = edge_weight * laplace + ridge_weight * mid
        base_ref[pl.ds(i, per)] = (
            u[pl.ds(i, per)].astype(F32)
            - 0.5 * step_pixel * prior
            + math.sqrt(step_pixel) * nz[pl.ds(i, per)].astype(F32)
        )
        return lax.dot_general(
            prior.astype(BF16).reshape(per * block, -1),
            cov[pl.ds(i, per)].reshape(per * block, cov.shape[2]),
            (((0,), (0,)), ((), ())),
            preferred_element_type=F32,
        )

    for k in range(parts):
        if k == 0:
            link_acc[...] = prior_rows(0)
        else:
            link_acc[...] += prior_rows(k * per)

    for j in range(1, nr):
        for k in range(nc):
            for c0 in (at.c0, 1 - at.c0):
                b = (at.r1_at(nr - j), at.r0, at.c1_at(nc - k), c0)
                arrive(b)
                pass_on(b, [at.core])
    lk[...] = link_acc[...].T.reshape(lk.shape)
    used = [0]
    pending = []

    def post(src, dst, device):
        k = used[0]
        used[0] += 1
        copy = send(src, dst, link_send.at[k], link_recv.at[k], device)
        pending.append(copy)
        return copy

    def settle(copies):
        for copy in copies:
            copy.wait_recv()

    hop = [post(lk.at[1 - at.r0], lk_core, at.core)]
    for j in range(nr):
        for k in range(nc):
            for c0 in (at.c0, 1 - at.c0):
                arrive((at.r1_at(nr - j), 1 - at.r0, at.c1_at(nc - k), c0))
    obs_load.wait()

    live = live_ref[0]
    day_blocks = days.shape[0] * days.shape[1] // block
    span = block // days.shape[1]
    slots = obs.shape[0]
    wide = 4
    stages = 7
    turns = slots // wide

    def turn(t, carry):
        for j in range(wide):
            slot = t * wide + j
            e = blocks_ref[slot]
            pb, db = e // day_blocks, lax.rem(e, day_blocks)
            uu = u[pb]
            vv = days[pl.ds(db * span, span)].reshape(block, u.shape[2])
            predicted = lax.dot_general(uu, vv, (((1,), (1,)), ((), ())), preferred_element_type=F32)
            residual = jnp.where(slot < live, obs[slot].astype(F32) - predicted, 0.0).astype(BF16)
            grad_ref[slot] = jnp.dot(residual, vv, preferred_element_type=F32).astype(BF16)
            term_ref[slot] = lax.dot_general(
                residual, uu, (((0,), (0,)), ((), ())), preferred_element_type=F32
            ).astype(BF16)
        return carry

    for stage in range(stages + 1):
        lax.fori_loop(stage * turns // (stages + 1), (stage + 1) * turns // (stages + 1), turn, 0)
        settle(hop)
        if stage == 0:
            lm_core[...] = lk[at.r0] + lk_core[...]
            hop = [post(lm_core.at[at.r1_at(k)], lk_x.at[k - 1], at.x_peer(k)) for k in range(1, nr)]
        elif stage == 1:
            link = lm_core[at.r1]
            for k in range(nr - 1):
                link = link + lk_x[k]
            lm_x[...] = link
            hop = [post(lm_x.at[1 - at.c0], lk_side, at.side)]
        elif stage == 2:
            lk_z[at.c1] = lm_x[at.c0] + lk_side[...]
            hop = [post(lk_z.at[at.c1], lk_z.at[at.c1], at.z_peer(k)) for k in range(1, nc)]
        elif stage == 3:
            link = lk_z[0]
            for k in range(1, nc):
                link = link + lk_z[k]
            total[at.r0, at.r1, at.c0] = link
            hop = [post(total.at[at.r0, at.r1, at.c0], total.at[at.r0, at.r1, at.c0], at.side)]
        elif stage == 4:
            hop = [post(total.at[at.r0, at.r1], total.at[at.r0, at.r1], at.x_peer(k)) for k in range(1, nr)]
        elif stage == 5:
            hop = [post(total.at[at.r0], total.at[at.r0], at.core)]
        else:
            hop = []
    for copy in sends + pending:
        copy.wait_send()


def run_field(rows, cols, blocks, live, factors_v, link_beta, covariates, factors_u, noise_u, obs):
    tile, block, rank = factors_u.shape
    covar = covariates.shape[2]
    per_device = factors_v.shape[0]
    slots = obs.shape[0]
    count = rows * cols
    nr, nc = rows // 2, cols // 2
    piece = covar // (4 * nr)
    lshape = (2, nr, 2, piece, rank)
    hops = 2 * (1 + (nr - 1) + 1) + (nc - 1)
    smem = pl.BlockSpec(memory_space=pltpu.SMEM)
    return pl.pallas_call(
        functools.partial(field_kernel, rows, cols),
        out_shape=(
            jax.ShapeDtypeStruct((tile, block, rank), F32),
            jax.ShapeDtypeStruct(lshape, F32),
            jax.ShapeDtypeStruct((slots, block, rank), BF16),
            jax.ShapeDtypeStruct((slots, block, rank), BF16),
        ),
        in_specs=[smem, smem, VMEM, VMEM, ANY, ANY, ANY, ANY],
        out_specs=(VMEM, VMEM, VMEM, VMEM),
        scratch_shapes=[
            pltpu.VMEM((count, per_device, rank), BF16),
            pltpu.VMEM((tile, block, covar), BF16),
            pltpu.VMEM((tile, block, rank), BF16),
            pltpu.VMEM((tile, block, rank), BF16),
            pltpu.VMEM((slots, block, block), BF16),
            pltpu.VMEM((covar, rank), BF16),
            pltpu.VMEM((tile + 2, block, rank), F32),
            pltpu.VMEM((2, tile, rank), F32),
            pltpu.VMEM((2, tile, rank), F32),
            pltpu.VMEM((rank, covar), F32),
            pltpu.VMEM(lshape, F32),
            pltpu.VMEM((nr, 2, piece, rank), F32),
            pltpu.VMEM((nr, 2, piece, rank), F32),
            pltpu.VMEM((nr - 1, 2, piece, rank), F32),
            pltpu.VMEM((2, piece, rank), F32),
            pltpu.VMEM((piece, rank), F32),
            pltpu.VMEM((nc, piece, rank), F32),
            pltpu.SemaphoreType.DMA((7,)),
            pltpu.SemaphoreType.DMA((count,)),
            pltpu.SemaphoreType.DMA((count,)),
            pltpu.SemaphoreType.DMA((4,)),
            pltpu.SemaphoreType.DMA((4,)),
            pltpu.SemaphoreType.DMA((hops,)),
            pltpu.SemaphoreType.DMA((hops,)),
        ],
        compiler_params=pltpu.CompilerParams(
            collective_id=0, has_side_effects=True, vmem_limit_bytes=LIMIT
        ),
    )(blocks, live, factors_v, link_beta, covariates, factors_u, noise_u, obs)


def add_kernel(day_blocks, step_link, blocks_ref, base_ref, grad_ref, term_ref, total_ref, beta_ref, nb_ref,
               next_ref, dv_ref, beta_out, acc_u, acc_v):
    acc_u[...] = base_ref[...]
    acc_v[...] = jnp.zeros_like(acc_v)
    wide = 4

    def turn(t, carry):
        for j in range(wide):
            slot = t * wide + j
            e = blocks_ref[slot]
            pb, db = e // day_blocks, lax.rem(e, day_blocks)
            acc_u[pb] += 0.5 * step_pixel * grad_ref[slot].astype(F32)
            acc_v[db] += term_ref[slot].astype(F32)
        return carry

    lax.fori_loop(0, grad_ref.shape[0] // wide, turn, 0)
    next_ref[...] = acc_u[...].astype(BF16)
    dv_ref[...] = acc_v[...].astype(BF16)
    old = beta_ref[...]
    beta_out[...] = old + 0.5 * step_link * (total_ref[...] - old) + math.sqrt(step_link) * nb_ref[...]


def run_add(day_blocks, step_link, blocks, base, grad, term, total, link_beta, noise_beta):
    tile, block, rank = base.shape
    return pl.pallas_call(
        functools.partial(add_kernel, day_blocks, step_link),
        out_shape=(
            jax.ShapeDtypeStruct((tile, block, rank), BF16),
            jax.ShapeDtypeStruct((day_blocks, block, rank), BF16),
            jax.ShapeDtypeStruct(link_beta.shape, F32),
        ),
        in_specs=[pl.BlockSpec(memory_space=pltpu.SMEM)] + [VMEM] * 6,
        out_specs=(VMEM, VMEM, VMEM),
        scratch_shapes=[
            pltpu.VMEM((tile, block, rank), F32),
            pltpu.VMEM((day_blocks, block, rank), F32),
        ],
        compiler_params=pltpu.CompilerParams(vmem_limit_bytes=LIMIT),
    )(blocks, base, grad, term, total, link_beta, noise_beta)


def sum_kernel(
    rows, cols, step_day, dv, fv_ref, nv_ref, v_ref,
    got_a, got_b, mid_a, mid_b, far_a, far_b, part_a, part_b, last_a, last_b, mid, got_z,
    send_sem, recv_sem,
):
    at = Place(rows, cols)
    nr, nc = at.nr, at.nc
    half = nc // 2
    greet(at.partners())
    used = [0]
    pending = []

    def post(src, dst, device):
        k = used[0]
        used[0] += 1
        copy = send(src, dst, send_sem.at[k], recv_sem.at[k], device)
        pending.append(copy)
        return copy

    def settle(copies):
        for copy in copies:
            copy.wait_recv()

    def summed(own, refs):
        part = own.astype(F32)
        for ref in refs:
            part = part + ref.astype(F32)
        return part

    first, second = pl.ds(0, half), pl.ds(half, half)
    a = [post(dv.at[:, 1 - at.r0, first], got_a, at.core)]
    b = [post(dv.at[:, 1 - at.r0, second], got_b, at.core)]
    settle(a)
    mid_a[...] = summed(dv[:, at.r0, first], [got_a[...]]).astype(BF16)
    a = [post(mid_a.at[at.r1_at(k)], far_a.at[k - 1], at.x_peer(k)) for k in range(1, nr)]
    settle(b)
    mid_b[...] = summed(dv[:, at.r0, second], [got_b[...]]).astype(BF16)
    b = [post(mid_b.at[:, :, 1 - at.c0], far_b, at.side)]
    settle(a)
    part_a[...] = summed(mid_a[at.r1], [far_a[k] for k in range(nr - 1)]).astype(BF16)
    a = [post(part_a.at[:, 1 - at.c0], last_a, at.side)]
    settle(b)
    part_b[...] = summed(mid_b[:, :, at.c0], [far_b[...]]).astype(BF16)
    b = [post(part_b.at[at.r1_at(k)], last_b.at[k - 1], at.x_peer(k)) for k in range(1, nr)]
    settle(a)
    mid[first] = summed(part_a[:, at.c0], [last_a[...]]).astype(BF16)
    settle(b)
    mid[second] = summed(part_b[at.r1], [last_b[k] for k in range(nr - 1)]).astype(BF16)
    a = [post(mid.at[at.c1_at(k)], got_z.at[k - 1], at.z_peer(k)) for k in range(1, nc)]
    settle(a)
    part = summed(mid[at.c1], [got_z[k] for k in range(nc - 1)])
    old = fv_ref[...]
    v_ref[...] = old + 0.5 * step_day * (part - old) + math.sqrt(step_day) * nv_ref[...]
    for copy in pending:
        copy.wait_send()


def run_sum(rows, cols, step_day, dv, factors_v, noise_v):
    nr, nc = rows // 2, cols // 2
    half = nc // 2
    per_device, rank = factors_v.shape
    sends = 2 * (1 + (nr - 1) + 1) + (nc - 1)
    buf = lambda *lead: pltpu.VMEM((*lead, per_device, rank), BF16)
    return pl.pallas_call(
        functools.partial(sum_kernel, rows, cols, step_day),
        out_shape=jax.ShapeDtypeStruct((per_device, rank), F32),
        in_specs=[VMEM] * 3,
        out_specs=VMEM,
        scratch_shapes=[
            buf(nr, half, 2), buf(nr, half, 2),
            buf(nr, half, 2), buf(nr, half, 2),
            buf(nr - 1, half, 2), buf(nr, half),
            buf(half, 2), buf(nr, half),
            buf(half), buf(nr - 1, half),
            buf(nc), buf(nc - 1),
            pltpu.SemaphoreType.DMA((sends,)),
            pltpu.SemaphoreType.DMA((sends,)),
        ],
        compiler_params=pltpu.CompilerParams(
            collective_id=1, has_side_effects=True, vmem_limit_bytes=LIMIT
        ),
    )(dv.reshape(nr, 2, nc, 2, per_device, rank), factors_v, noise_v)


def shards(
    factors_u, covariates, link_beta, factors_v, obs_values, obs_blocks, obs_count,
    noise_u, noise_v, noise_beta,
):
    rows = lax.axis_size("row")
    cols = lax.axis_size("col")
    devices = rows * cols
    tile, block, rank = factors_u.shape
    per_device = factors_v.shape[0]
    days = per_device * devices
    day_blocks = days // block
    slots = obs_blocks.shape[1]
    step_day = 0.25 / math.sqrt(devices * slots * block / day_blocks)
    step_link = 0.25 / math.sqrt(devices * tile * block)
    base, total, grad, term = run_field(
        rows, cols, obs_blocks[0], obs_count, factors_v, link_beta, covariates, factors_u, noise_u,
        obs_values[0],
    )
    u_next, dv, beta_next = run_add(
        day_blocks, step_link, obs_blocks[0], base, grad, term,
        total.reshape(link_beta.shape), link_beta, noise_beta,
    )
    v_next = run_sum(rows, cols, step_day, dv, factors_v, noise_v)
    return (u_next, v_next, beta_next)


def solution(mesh):
    in_specs = (
        P("row", "col", None),
        P("row", "col", None),
        P(),
        P(("row", "col"), None),
        P(("row", "col"), None, None, None),
        P(("row", "col"), None),
        P(("row", "col")),
        P("row", "col", None),
        P(("row", "col"), None),
        P(),
    )
    out_specs = (P("row", "col", None), P(("row", "col"), None), P())
    return jax.shard_map(shards, mesh=mesh, in_specs=in_specs, out_specs=out_specs, check_vma=False)
```

```python
import functools
import math

import jax
import jax.numpy as jnp
from jax import lax
from jax.experimental import pallas as pl
from jax.experimental.pallas import tpu as pltpu
from jax.sharding import PartitionSpec as P

edge_weight = 0.5
ridge_weight = 0.1
step_pixel = 0.2
MESH = pl.DeviceIdType.MESH
F32 = jnp.float32
BF16 = jnp.bfloat16
VMEM = pl.BlockSpec(memory_space=pltpu.VMEM)
HBM = pl.BlockSpec(memory_space=pltpu.HBM)
LIMIT = 40 * 1024 * 1024
LIMIT_FIELD = 40 * 1024 * 1024


class Place:
    def __init__(self, rows, cols):
        self.rows, self.cols = rows, cols
        self.nr, self.nc = rows // 2, cols // 2
        self.r, self.c = lax.axis_index("row"), lax.axis_index("col")
        self.r1, self.r0 = self.r // 2, lax.rem(self.r, 2)
        self.c1, self.c0 = self.c // 2, lax.rem(self.c, 2)
        self.core = (self.r1 * 2 + (1 - self.r0), self.c)
        self.side = (self.r, self.c1 * 2 + (1 - self.c0))

    def r1_at(self, k):
        return lax.rem(self.r1 + k, self.nr)

    def c1_at(self, k):
        return lax.rem(self.c1 + k, self.nc)

    def x_peer(self, k):
        return (self.r1_at(k) * 2 + self.r0, self.c)

    def z_peer(self, k):
        return (self.r, self.c1_at(k) * 2 + self.c0)

    def quad(self):
        found = []
        for k in range(self.nr):
            for c0 in (self.c0, 1 - self.c0):
                if k or c0 is not self.c0:
                    r1 = self.r1_at(k)
                    found.append(((r1 * 2 + self.r0, self.c1 * 2 + c0), r1, c0))
        return found

    def partners(self):
        return (
            [self.core, self.side]
            + [self.x_peer(k) for k in range(1, self.nr)]
            + [self.z_peer(k) for k in range(1, self.nc)]
        )


def greet(partners):
    barrier = pltpu.get_barrier_semaphore()
    for partner in partners:
        pl.semaphore_signal(barrier, inc=1, device_id=partner, device_id_type=MESH)
    pl.semaphore_wait(barrier, len(partners))


def send(src, dst, send_sem, recv_sem, device):
    copy = pltpu.make_async_remote_copy(
        src_ref=src, dst_ref=dst, send_sem=send_sem, recv_sem=recv_sem,
        device_id=device, device_id_type=MESH,
    )
    copy.start()
    return copy


def field_kernel(
    rows, cols, blocks_ref, live_ref, fv_ref, beta_ref, cov_hbm, u_hbm, nz_hbm, obs_hbm,
    base_ref, total, grad_ref, term_ref,
    days, cov, u, nz, obs, beta, rp, edge_send, edge_recv, link_acc,
    lk, lk_core, lm_core, lk_quad, lk_z, fv, beta_wide,
    load_sem, day_send, day_recv, halo_send, halo_recv, link_send, link_recv,
):
    at = Place(rows, cols)
    nr, nc = at.nr, at.nc
    tile, block = u.shape[0], u.shape[1]
    parts = 4
    per = tile // parts
    loads = []
    for k in range(parts):
        loads.append(pltpu.make_async_copy(cov_hbm.at[pl.ds(k * per, per)], cov.at[pl.ds(k * per, per)], load_sem.at[k]))
    u_load = pltpu.make_async_copy(u_hbm, u, load_sem.at[parts])
    nz_load = pltpu.make_async_copy(nz_hbm, nz, load_sem.at[parts + 1])
    fv_load = pltpu.make_async_copy(fv_ref, fv, load_sem.at[parts + 3])
    beta_load = pltpu.make_async_copy(beta_ref, beta_wide, load_sem.at[parts + 4])
    fv_load.start()
    beta_load.start()
    loads[0].start()
    u_load.start()
    for load in loads[1:]:
        load.start()
    nz_load.start()
    obs_load = pltpu.make_async_copy(obs_hbm, obs, load_sem.at[parts + 2])
    obs_load.start()

    def index_of(b):
        return ((b[0] * 2 + b[1]) * nc + b[2]) * 2 + b[3]

    fv_load.wait()
    days[at.r * cols + at.c] = fv[...].astype(BF16)
    north = (lax.rem(at.r + rows - 1, rows), at.c)
    south = (lax.rem(at.r + 1, rows), at.c)
    west = (at.r, lax.rem(at.c + cols - 1, cols))
    east = (at.r, lax.rem(at.c + 1, cols))
    quad = at.quad()
    greet(
        [at.core] + [q[0] for q in quad] + [at.z_peer(k) for k in range(1, nc)]
        + [north, south, west, east]
    )

    sends = []

    def block_at(b):
        return days.at[index_of(b)]

    def sem_at(b):
        return day_recv.at[index_of(b)]

    def pass_on(b, partners):
        for partner in partners:
            sends.append(send(block_at(b), block_at(b), day_send.at[len(sends)], sem_at(b), partner))

    def arrive(b):
        pltpu.make_async_remote_copy(
            src_ref=block_at(b), dst_ref=block_at(b), send_sem=day_send.at[0], recv_sem=sem_at(b),
            device_id=at.core, device_id_type=MESH,
        ).wait_recv()

    zs = [at.z_peer(k) for k in range(1, nc)]
    xs = [at.x_peer(k) for k in range(1, nr)]
    own = (at.r1, at.r0, at.c1, at.c0)
    pass_on(own, zs + [at.side] + xs + [at.core])

    beta_load.wait()
    beta[...] = beta_wide[...].astype(BF16)

    def resid_rows(i):
        cells = cov[pl.ds(i, per)].reshape(per * block, cov.shape[2])
        mean = jnp.dot(cells, beta[...], preferred_element_type=F32)
        rp[pl.ds(i + 1, per)] = u[pl.ds(i, per)].astype(F32) - mean.reshape(per, block, -1)

    u_load.wait()
    for k in range(parts):
        loads[k].wait()
        resid_rows(k * per)
    edge_send[0] = rp[pl.ds(1, tile), 0, :]
    edge_send[1] = rp[pl.ds(1, tile), block - 1, :]
    halos = [
        send(rp.at[1], rp.at[tile + 1], halo_send.at[0], halo_recv.at[0], north),
        send(rp.at[tile], rp.at[0], halo_send.at[1], halo_recv.at[1], south),
        send(edge_send.at[0], edge_recv.at[1], halo_send.at[2], halo_recv.at[2], west),
        send(edge_send.at[1], edge_recv.at[0], halo_send.at[3], halo_recv.at[3], east),
    ]

    for k in range(1, nc):
        b = (at.r1, at.r0, at.c1_at(nc - k), at.c0)
        arrive(b)
        pass_on(b, [at.side] + xs + [at.core])
    for k in range(nc):
        b = (at.r1, at.r0, at.c1_at(nc - k), 1 - at.c0)
        arrive(b)
        pass_on(b, xs + [at.core])

    nz_load.wait()
    for halo in halos:
        halo.wait()
    for spot, gone in ((0, at.r == 0), (tile + 1, at.r == rows - 1)):
        rp[spot] = jnp.where(gone, 0.0, rp[spot])
    for spot, gone in ((0, at.c == 0), (1, at.c == cols - 1)):
        edge_recv[spot] = jnp.where(gone, 0.0, edge_recv[spot])

    lane_row = lax.broadcasted_iota(jnp.int32, (per, block, u.shape[2]), 1)

    def prior_rows(i):
        mid = rp[pl.ds(i + 1, per)]
        around = rp[pl.ds(i, per)] + rp[pl.ds(i + 2, per)]
        left = jnp.where(lane_row == 0, edge_recv[0, pl.ds(i, per)][:, None, :], pltpu.roll(mid, 1, 1))
        right = jnp.where(
            lane_row == block - 1, edge_recv[1, pl.ds(i, per)][:, None, :], pltpu.roll(mid, block - 1, 1)
        )
        laplace = 4.0 * mid - (around + right + left)
        prior = edge_weight * laplace + ridge_weight * mid
        base_ref[pl.ds(i, per)] = (
            u[pl.ds(i, per)].astype(F32)
            - 0.5 * step_pixel * prior
            + math.sqrt(step_pixel) * nz[pl.ds(i, per)].astype(F32)
        )
        return lax.dot_general(
            prior.astype(BF16).reshape(per * block, -1),
            cov[pl.ds(i, per)].reshape(per * block, cov.shape[2]),
            (((0,), (0,)), ((), ())),
            preferred_element_type=F32,
        )

    for k in range(parts):
        if k == 0:
            link_acc[...] = prior_rows(0)
        else:
            link_acc[...] += prior_rows(k * per)

    for j in range(1, nr):
        for k in range(nc):
            for c0 in (at.c0, 1 - at.c0):
                b = (at.r1_at(nr - j), at.r0, at.c1_at(nc - k), c0)
                arrive(b)
                pass_on(b, [at.core])
    lk[...] = link_acc[...].T.reshape(lk.shape)
    used = [0]
    pending = []

    def post(src, dst, device):
        k = used[0]
        used[0] += 1
        copy = send(src, dst, link_send.at[k], link_recv.at[k], device)
        pending.append(copy)
        return copy

    def settle(copies):
        for copy in copies:
            copy.wait_recv()

    hop = [post(lk.at[1 - at.r0], lk_core, at.core)]
    for j in range(nr):
        for k in range(nc):
            for c0 in (at.c0, 1 - at.c0):
                arrive((at.r1_at(nr - j), 1 - at.r0, at.c1_at(nc - k), c0))
    obs_load.wait()

    live = live_ref[0]
    day_blocks = days.shape[0] * days.shape[1] // block
    span = block // days.shape[1]
    slots = obs.shape[0]
    wide = 16
    stages = 5
    turns = slots // wide

    def turn(t, carry):
        taken = []
        for j in range(wide):
            slot = t * wide + j
            e = blocks_ref[slot]
            pb, db = e // day_blocks, lax.rem(e, day_blocks)
            taken.append((slot, u[pb], days[pl.ds(db * span, span)].reshape(block, u.shape[2]), obs[slot]))
        resid = []
        for slot, uu, vv, yy in taken:
            predicted = lax.dot_general(uu, vv, (((1,), (1,)), ((), ())), preferred_element_type=F32)
            resid.append(jnp.where(slot < live, yy.astype(F32) - predicted, 0.0).astype(BF16))
        grads = [
            jnp.dot(res, vv, preferred_element_type=F32).astype(BF16)
            for res, (_, _, vv, _) in zip(resid, taken)
        ]
        terms = [
            lax.dot_general(res, uu, (((0,), (0,)), ((), ())), preferred_element_type=F32).astype(BF16)
            for res, (_, uu, _, _) in zip(resid, taken)
        ]
        for (slot, _, _, _), grad, term in zip(taken, grads, terms):
            grad_ref[slot] = grad
            term_ref[slot] = term
        return carry

    for stage in range(stages + 1):
        lax.fori_loop(stage * turns // (stages + 1), (stage + 1) * turns // (stages + 1), turn, 0)
        settle(hop)
        if stage == 0:
            lm_core[...] = lk[at.r0] + lk_core[...]
            hop = [
                post(lm_core.at[r1, c0], lk_quad.at[q], device)
                for q, (device, r1, c0) in enumerate(quad)
            ]
        elif stage == 1:
            link = lm_core[at.r1, at.c0]
            for q in range(len(quad)):
                link = link + lk_quad[q]
            lk_z[at.c1] = link
            hop = [post(lk_z.at[at.c1], lk_z.at[at.c1], at.z_peer(k)) for k in range(1, nc)]
        elif stage == 2:
            link = lk_z[0]
            for k in range(1, nc):
                link = link + lk_z[k]
            own_piece = total.at[at.r0, at.r1, at.c0]
            own_piece[...] = link
            hop = [post(own_piece, own_piece, device) for device, _, _ in quad]
        elif stage == 3:
            hop = [post(total.at[at.r0], total.at[at.r0], at.core)]
        else:
            hop = []
    for copy in sends + pending:
        copy.wait_send()


def run_field(rows, cols, blocks, live, factors_v, link_beta, covariates, factors_u, noise_u, obs):
    tile, block, rank = factors_u.shape
    covar = covariates.shape[2]
    per_device = factors_v.shape[0]
    slots = obs.shape[0]
    count = rows * cols
    nr, nc = rows // 2, cols // 2
    piece = covar // (4 * nr)
    lshape = (2, nr, 2, piece, rank)
    quad = 2 * nr - 1
    hops = 2 * (1 + quad) + (nc - 1)
    smem = pl.BlockSpec(memory_space=pltpu.SMEM)
    return pl.pallas_call(
        functools.partial(field_kernel, rows, cols),
        out_shape=(
            jax.ShapeDtypeStruct((tile, block, rank), F32),
            jax.ShapeDtypeStruct(lshape, F32),
            jax.ShapeDtypeStruct((slots, block, rank), BF16),
            jax.ShapeDtypeStruct((slots, block, rank), BF16),
        ),
        in_specs=[smem, smem, HBM, HBM, HBM, HBM, HBM, HBM],
        out_specs=(VMEM, VMEM, VMEM, VMEM),
        scratch_shapes=[
            pltpu.VMEM((count, per_device, rank), BF16),
            pltpu.VMEM((tile, block, covar), BF16),
            pltpu.VMEM((tile, block, rank), BF16),
            pltpu.VMEM((tile, block, rank), BF16),
            pltpu.VMEM((slots, block, block), BF16),
            pltpu.VMEM((covar, rank), BF16),
            pltpu.VMEM((tile + 2, block, rank), F32),
            pltpu.VMEM((2, tile, rank), F32),
            pltpu.VMEM((2, tile, rank), F32),
            pltpu.VMEM((rank, covar), F32),
            pltpu.VMEM(lshape, F32),
            pltpu.VMEM((nr, 2, piece, rank), F32),
            pltpu.VMEM((nr, 2, piece, rank), F32),
            pltpu.VMEM((quad, piece, rank), F32),
            pltpu.VMEM((nc, piece, rank), F32),
            pltpu.VMEM((per_device, rank), F32),
            pltpu.VMEM((covar, rank), F32),
            pltpu.SemaphoreType.DMA((9,)),
            pltpu.SemaphoreType.DMA((count,)),
            pltpu.SemaphoreType.DMA((count,)),
            pltpu.SemaphoreType.DMA((4,)),
            pltpu.SemaphoreType.DMA((4,)),
            pltpu.SemaphoreType.DMA((hops,)),
            pltpu.SemaphoreType.DMA((hops,)),
        ],
        compiler_params=pltpu.CompilerParams(
            collective_id=0, has_side_effects=True, vmem_limit_bytes=LIMIT_FIELD
        ),
    )(blocks, live, factors_v, link_beta, covariates, factors_u, noise_u, obs)


def add_kernel(day_blocks, step_link, blocks_ref, base_ref, grad_ref, term_ref, total_ref, beta_ref, nb_ref,
               next_ref, dv_ref, beta_out, acc_u, acc_v):
    acc_u[...] = base_ref[...]
    acc_v[...] = jnp.zeros_like(acc_v)
    wide = 4

    def turn(t, carry):
        for j in range(wide):
            slot = t * wide + j
            e = blocks_ref[slot]
            pb, db = e // day_blocks, lax.rem(e, day_blocks)
            acc_u[pb] += 0.5 * step_pixel * grad_ref[slot].astype(F32)
            acc_v[db] += term_ref[slot].astype(F32)
        return carry

    lax.fori_loop(0, grad_ref.shape[0] // wide, turn, 0)
    next_ref[...] = acc_u[...].astype(BF16)
    dv_ref[...] = acc_v[...].astype(BF16)
    old = beta_ref[...]
    beta_out[...] = old + 0.5 * step_link * (total_ref[...] - old) + math.sqrt(step_link) * nb_ref[...]


def run_add(day_blocks, step_link, blocks, base, grad, term, total, link_beta, noise_beta):
    tile, block, rank = base.shape
    return pl.pallas_call(
        functools.partial(add_kernel, day_blocks, step_link),
        out_shape=(
            jax.ShapeDtypeStruct((tile, block, rank), BF16),
            jax.ShapeDtypeStruct((day_blocks, block, rank), BF16),
            jax.ShapeDtypeStruct(link_beta.shape, F32),
        ),
        in_specs=[pl.BlockSpec(memory_space=pltpu.SMEM)] + [VMEM] * 6,
        out_specs=(VMEM, VMEM, VMEM),
        scratch_shapes=[
            pltpu.VMEM((tile, block, rank), F32),
            pltpu.VMEM((day_blocks, block, rank), F32),
        ],
        compiler_params=pltpu.CompilerParams(vmem_limit_bytes=LIMIT),
    )(blocks, base, grad, term, total, link_beta, noise_beta)


def sum_kernel(
    rows, cols, step_day, dv, fv_ref, nv_ref, v_ref,
    got_a, got_b, mid_a, mid_b, far_a, far_b, part_a, part_b, last_a, last_b, mid, got_z,
    send_sem, recv_sem,
):
    at = Place(rows, cols)
    nr, nc = at.nr, at.nc
    half = nc // 2
    greet(at.partners())
    used = [0]
    pending = []

    def post(src, dst, device):
        k = used[0]
        used[0] += 1
        copy = send(src, dst, send_sem.at[k], recv_sem.at[k], device)
        pending.append(copy)
        return copy

    def settle(copies):
        for copy in copies:
            copy.wait_recv()

    def summed(own, refs):
        part = own.astype(F32)
        for ref in refs:
            part = part + ref.astype(F32)
        return part

    first, second = pl.ds(0, half), pl.ds(half, half)
    a = [post(dv.at[:, 1 - at.r0, first], got_a, at.core)]
    b = [post(dv.at[:, 1 - at.r0, second], got_b, at.core)]
    settle(a)
    mid_a[...] = summed(dv[:, at.r0, first], [got_a[...]]).astype(BF16)
    a = [post(mid_a.at[at.r1_at(k)], far_a.at[k - 1], at.x_peer(k)) for k in range(1, nr)]
    settle(b)
    mid_b[...] = summed(dv[:, at.r0, second], [got_b[...]]).astype(BF16)
    b = [post(mid_b.at[:, :, 1 - at.c0], far_b, at.side)]
    settle(a)
    part_a[...] = summed(mid_a[at.r1], [far_a[k] for k in range(nr - 1)]).astype(BF16)
    a = [post(part_a.at[:, 1 - at.c0], last_a, at.side)]
    settle(b)
    part_b[...] = summed(mid_b[:, :, at.c0], [far_b[...]]).astype(BF16)
    b = [post(part_b.at[at.r1_at(k)], last_b.at[k - 1], at.x_peer(k)) for k in range(1, nr)]
    settle(a)
    mid[first] = summed(part_a[:, at.c0], [last_a[...]]).astype(BF16)
    settle(b)
    mid[second] = summed(part_b[at.r1], [last_b[k] for k in range(nr - 1)]).astype(BF16)
    a = [post(mid.at[at.c1_at(k)], got_z.at[k - 1], at.z_peer(k)) for k in range(1, nc)]
    settle(a)
    part = summed(mid[at.c1], [got_z[k] for k in range(nc - 1)])
    old = fv_ref[...]
    v_ref[...] = old + 0.5 * step_day * (part - old) + math.sqrt(step_day) * nv_ref[...]
    for copy in pending:
        copy.wait_send()


def run_sum(rows, cols, step_day, dv, factors_v, noise_v):
    nr, nc = rows // 2, cols // 2
    half = nc // 2
    per_device, rank = factors_v.shape
    sends = 2 * (1 + (nr - 1) + 1) + (nc - 1)
    buf = lambda *lead: pltpu.VMEM((*lead, per_device, rank), BF16)
    return pl.pallas_call(
        functools.partial(sum_kernel, rows, cols, step_day),
        out_shape=jax.ShapeDtypeStruct((per_device, rank), F32),
        in_specs=[VMEM] * 3,
        out_specs=VMEM,
        scratch_shapes=[
            buf(nr, half, 2), buf(nr, half, 2),
            buf(nr, half, 2), buf(nr, half, 2),
            buf(nr - 1, half, 2), buf(nr, half),
            buf(half, 2), buf(nr, half),
            buf(half), buf(nr - 1, half),
            buf(nc), buf(nc - 1),
            pltpu.SemaphoreType.DMA((sends,)),
            pltpu.SemaphoreType.DMA((sends,)),
        ],
        compiler_params=pltpu.CompilerParams(
            collective_id=1, has_side_effects=True, vmem_limit_bytes=LIMIT
        ),
    )(dv.reshape(nr, 2, nc, 2, per_device, rank), factors_v, noise_v)


def shards(
    factors_u, covariates, link_beta, factors_v, obs_values, obs_blocks, obs_count,
    noise_u, noise_v, noise_beta,
):
    rows = lax.axis_size("row")
    cols = lax.axis_size("col")
    devices = rows * cols
    tile, block, rank = factors_u.shape
    per_device = factors_v.shape[0]
    days = per_device * devices
    day_blocks = days // block
    slots = obs_blocks.shape[1]
    step_day = 0.25 / math.sqrt(devices * slots * block / day_blocks)
    step_link = 0.25 / math.sqrt(devices * tile * block)
    base, total, grad, term = run_field(
        rows, cols, obs_blocks[0], obs_count, factors_v, link_beta, covariates, factors_u, noise_u,
        obs_values[0],
    )
    u_next, dv, beta_next = run_add(
        day_blocks, step_link, obs_blocks[0], base, grad, term,
        total.reshape(link_beta.shape), link_beta, noise_beta,
    )
    v_next = run_sum(rows, cols, step_day, dv, factors_v, noise_v)
    return (u_next, v_next, beta_next)


def solution(mesh):
    in_specs = (
        P("row", "col", None),
        P("row", "col", None),
        P(),
        P(("row", "col"), None),
        P(("row", "col"), None, None, None),
        P(("row", "col"), None),
        P(("row", "col")),
        P("row", "col", None),
        P(("row", "col"), None),
        P(),
    )
    out_specs = (P("row", "col", None), P(("row", "col"), None), P())
    return jax.shard_map(shards, mesh=mesh, in_specs=in_specs, out_specs=out_specs, check_vma=False)
```

```python
import functools
import math

import jax
import jax.numpy as jnp
from jax import lax
from jax.experimental import pallas as pl
from jax.experimental.pallas import tpu as pltpu
from jax.sharding import PartitionSpec as P

edge_weight = 0.5
ridge_weight = 0.1
step_pixel = 0.2
MESH = pl.DeviceIdType.MESH
F32 = jnp.float32
BF16 = jnp.bfloat16
VMEM = pl.BlockSpec(memory_space=pltpu.VMEM)
HBM = pl.BlockSpec(memory_space=pltpu.HBM)
LIMIT = 40 * 1024 * 1024
LIMIT_FIELD = 40 * 1024 * 1024


class Place:
    def __init__(self, rows, cols):
        self.rows, self.cols = rows, cols
        self.nr, self.nc = rows // 2, cols // 2
        self.r, self.c = lax.axis_index("row"), lax.axis_index("col")
        self.r1, self.r0 = self.r // 2, lax.rem(self.r, 2)
        self.c1, self.c0 = self.c // 2, lax.rem(self.c, 2)
        self.core = (self.r1 * 2 + (1 - self.r0), self.c)
        self.side = (self.r, self.c1 * 2 + (1 - self.c0))

    def r1_at(self, k):
        return lax.rem(self.r1 + k, self.nr)

    def c1_at(self, k):
        return lax.rem(self.c1 + k, self.nc)

    def x_peer(self, k):
        return (self.r1_at(k) * 2 + self.r0, self.c)

    def z_peer(self, k):
        return (self.r, self.c1_at(k) * 2 + self.c0)

    def quad(self):
        found = []
        for k in range(self.nr):
            for c0 in (self.c0, 1 - self.c0):
                if k or c0 is not self.c0:
                    r1 = self.r1_at(k)
                    found.append(((r1 * 2 + self.r0, self.c1 * 2 + c0), r1, c0))
        return found

    def partners(self):
        return (
            [self.core, self.side]
            + [self.x_peer(k) for k in range(1, self.nr)]
            + [self.z_peer(k) for k in range(1, self.nc)]
        )


def greet(partners):
    barrier = pltpu.get_barrier_semaphore()
    for partner in partners:
        pl.semaphore_signal(barrier, inc=1, device_id=partner, device_id_type=MESH)
    pl.semaphore_wait(barrier, len(partners))


def send(src, dst, send_sem, recv_sem, device):
    copy = pltpu.make_async_remote_copy(
        src_ref=src, dst_ref=dst, send_sem=send_sem, recv_sem=recv_sem,
        device_id=device, device_id_type=MESH,
    )
    copy.start()
    return copy


def field_kernel(
    rows, cols, blocks_ref, live_ref, fv_ref, beta_ref, cov_hbm, u_hbm, nz_hbm, obs_hbm,
    base_ref, total, grad_ref, term_ref,
    days, cov, u, nz, obs, beta, rp, edge_send, edge_recv, link_acc,
    lk, lk_core, lm_core, lk_quad, lk_z,
    load_sem, day_send, day_recv, halo_send, halo_recv, link_send, link_recv,
):
    at = Place(rows, cols)
    nr, nc = at.nr, at.nc
    tile, block = u.shape[0], u.shape[1]
    parts = 4
    per = tile // parts
    loads = []
    for k in range(parts):
        loads.append(pltpu.make_async_copy(cov_hbm.at[pl.ds(k * per, per)], cov.at[pl.ds(k * per, per)], load_sem.at[k]))
    u_load = pltpu.make_async_copy(u_hbm, u, load_sem.at[parts])
    nz_load = pltpu.make_async_copy(nz_hbm, nz, load_sem.at[parts + 1])
    loads[0].start()
    u_load.start()
    for load in loads[1:]:
        load.start()
    nz_load.start()
    obs_load = pltpu.make_async_copy(obs_hbm, obs, load_sem.at[parts + 2])
    obs_load.start()

    def index_of(b):
        return ((b[0] * 2 + b[1]) * nc + b[2]) * 2 + b[3]

    days[at.r * cols + at.c] = fv_ref[...].astype(BF16)
    north = (lax.rem(at.r + rows - 1, rows), at.c)
    south = (lax.rem(at.r + 1, rows), at.c)
    west = (at.r, lax.rem(at.c + cols - 1, cols))
    east = (at.r, lax.rem(at.c + 1, cols))
    quad = at.quad()
    greet(
        [at.core] + [q[0] for q in quad] + [at.z_peer(k) for k in range(1, nc)]
        + [north, south, west, east]
    )

    sends = []

    def block_at(b):
        return days.at[index_of(b)]

    def sem_at(b):
        return day_recv.at[index_of(b)]

    def pass_on(b, partners):
        for partner in partners:
            sends.append(send(block_at(b), block_at(b), day_send.at[len(sends)], sem_at(b), partner))

    def arrive(b):
        pltpu.make_async_remote_copy(
            src_ref=block_at(b), dst_ref=block_at(b), send_sem=day_send.at[0], recv_sem=sem_at(b),
            device_id=at.core, device_id_type=MESH,
        ).wait_recv()

    zs = [at.z_peer(k) for k in range(1, nc)]
    xs = [at.x_peer(k) for k in range(1, nr)]
    own = (at.r1, at.r0, at.c1, at.c0)
    pass_on(own, zs + [at.side] + xs + [at.core])

    beta[...] = beta_ref[...].astype(BF16)

    def resid_rows(i):
        cells = cov[pl.ds(i, per)].reshape(per * block, cov.shape[2])
        mean = jnp.dot(cells, beta[...], preferred_element_type=F32)
        rp[pl.ds(i + 1, per)] = u[pl.ds(i, per)].astype(F32) - mean.reshape(per, block, -1)

    u_load.wait()
    for k in range(parts):
        loads[k].wait()
        resid_rows(k * per)
    edge_send[0] = rp[pl.ds(1, tile), 0, :]
    edge_send[1] = rp[pl.ds(1, tile), block - 1, :]
    halos = [
        send(rp.at[1], rp.at[tile + 1], halo_send.at[0], halo_recv.at[0], north),
        send(rp.at[tile], rp.at[0], halo_send.at[1], halo_recv.at[1], south),
        send(edge_send.at[0], edge_recv.at[1], halo_send.at[2], halo_recv.at[2], west),
        send(edge_send.at[1], edge_recv.at[0], halo_send.at[3], halo_recv.at[3], east),
    ]

    for k in range(1, nc):
        b = (at.r1, at.r0, at.c1_at(nc - k), at.c0)
        arrive(b)
        pass_on(b, [at.side] + xs + [at.core])
    for k in range(nc):
        b = (at.r1, at.r0, at.c1_at(nc - k), 1 - at.c0)
        arrive(b)
        pass_on(b, (xs if k % 2 == 0 else []) + [at.core])

    nz_load.wait()
    for halo in halos:
        halo.wait()
    for spot, gone in ((0, at.r == 0), (tile + 1, at.r == rows - 1)):
        rp[spot] = jnp.where(gone, 0.0, rp[spot])
    for spot, gone in ((0, at.c == 0), (1, at.c == cols - 1)):
        edge_recv[spot] = jnp.where(gone, 0.0, edge_recv[spot])

    lane_row = lax.broadcasted_iota(jnp.int32, (per, block, u.shape[2]), 1)

    def prior_rows(i):
        mid = rp[pl.ds(i + 1, per)]
        around = rp[pl.ds(i, per)] + rp[pl.ds(i + 2, per)]
        left = jnp.where(lane_row == 0, edge_recv[0, pl.ds(i, per)][:, None, :], pltpu.roll(mid, 1, 1))
        right = jnp.where(
            lane_row == block - 1, edge_recv[1, pl.ds(i, per)][:, None, :], pltpu.roll(mid, block - 1, 1)
        )
        laplace = 4.0 * mid - (around + right + left)
        prior = edge_weight * laplace + ridge_weight * mid
        base_ref[pl.ds(i, per)] = (
            u[pl.ds(i, per)].astype(F32)
            - 0.5 * step_pixel * prior
            + math.sqrt(step_pixel) * nz[pl.ds(i, per)].astype(F32)
        )
        return lax.dot_general(
            prior.astype(BF16).reshape(per * block, -1),
            cov[pl.ds(i, per)].reshape(per * block, cov.shape[2]),
            (((0,), (0,)), ((), ())),
            preferred_element_type=F32,
        )

    for k in range(parts):
        if k == 0:
            link_acc[...] = prior_rows(0)
        else:
            link_acc[...] += prior_rows(k * per)

    lk[...] = link_acc[...].T.reshape(lk.shape)
    used = [0]
    pending = []

    def post(src, dst, device):
        k = used[0]
        used[0] += 1
        copy = send(src, dst, link_send.at[k], link_recv.at[k], device)
        pending.append(copy)
        return copy

    def settle(copies):
        for copy in copies:
            copy.wait_recv()

    hop = [post(lk.at[1 - at.r0], lk_core, at.core)]
    for j in range(1, nr):
        for k in range(nc):
            b = (at.r1_at(nr - j), at.r0, at.c1_at(nc - k), at.c0)
            arrive(b)
            pass_on(b, ([at.side] if k % 2 else []) + [at.core])
    settle(hop)
    lm_core[...] = lk[at.r0] + lk_core[...]
    hop = [
        post(lm_core.at[r1, c0], lk_quad.at[q], device)
        for q, (device, r1, c0) in enumerate(quad)
    ]
    for j in range(1, nr):
        for k in range(nc):
            b = (at.r1_at(nr - j), at.r0, at.c1_at(nc - k), 1 - at.c0)
            arrive(b)
            pass_on(b, [at.core])
    for j in range(nr):
        for k in range(nc):
            for c0 in (at.c0, 1 - at.c0):
                arrive((at.r1_at(nr - j), 1 - at.r0, at.c1_at(nc - k), c0))
    obs_load.wait()

    live = live_ref[0]
    day_blocks = days.shape[0] * days.shape[1] // block
    span = block // days.shape[1]
    slots = obs.shape[0]
    wide = 16
    stages = 3
    turns = slots // wide

    def turn(t, carry):
        taken = []
        for j in range(wide):
            slot = t * wide + j
            e = blocks_ref[0, slot]
            pb, db = e // day_blocks, lax.rem(e, day_blocks)
            taken.append((slot, u[pb], days[pl.ds(db * span, span)].reshape(block, u.shape[2]), obs[slot]))
        resid = []
        for slot, uu, vv, yy in taken:
            predicted = lax.dot_general(uu, vv, (((1,), (1,)), ((), ())), preferred_element_type=F32)
            resid.append(jnp.where(slot < live, yy.astype(F32) - predicted, 0.0).astype(BF16))
        grads = [
            jnp.dot(res, vv, preferred_element_type=F32).astype(BF16)
            for res, (_, _, vv, _) in zip(resid, taken)
        ]
        terms = [
            lax.dot_general(res, uu, (((0,), (0,)), ((), ())), preferred_element_type=F32).astype(BF16)
            for res, (_, uu, _, _) in zip(resid, taken)
        ]
        for (slot, _, _, _), grad, term in zip(taken, grads, terms):
            grad_ref[slot] = grad
            term_ref[slot] = term
        return carry

    for stage in range(stages + 1):
        lax.fori_loop(stage * turns // (stages + 1), (stage + 1) * turns // (stages + 1), turn, 0)
        settle(hop)
        if stage == 0:
            link = lm_core[at.r1, at.c0]
            for q in range(len(quad)):
                link = link + lk_quad[q]
            lk_z[at.c1] = link
            hop = [post(lk_z.at[at.c1], lk_z.at[at.c1], at.z_peer(k)) for k in range(1, nc)]
        elif stage == 1:
            link = lk_z[0]
            for k in range(1, nc):
                link = link + lk_z[k]
            own_piece = total.at[at.r0, at.r1, at.c0]
            own_piece[...] = link
            hop = [post(own_piece, own_piece, device) for device, _, _ in quad]
        elif stage == 2:
            hop = [post(total.at[at.r0], total.at[at.r0], at.core)]
        else:
            hop = []
    for copy in sends + pending:
        copy.wait_send()


def run_field(rows, cols, blocks, live, factors_v, link_beta, covariates, factors_u, noise_u, obs):
    tile, block, rank = factors_u.shape
    covar = covariates.shape[2]
    per_device = factors_v.shape[0]
    slots = obs.shape[0]
    count = rows * cols
    nr, nc = rows // 2, cols // 2
    piece = covar // (4 * nr)
    lshape = (2, nr, 2, piece, rank)
    quad = 2 * nr - 1
    hops = 2 * (1 + quad) + (nc - 1)
    smem = pl.BlockSpec(memory_space=pltpu.SMEM)
    return pl.pallas_call(
        functools.partial(field_kernel, rows, cols),
        out_shape=(
            jax.ShapeDtypeStruct((tile, block, rank), F32),
            jax.ShapeDtypeStruct(lshape, F32),
            jax.ShapeDtypeStruct((slots, block, rank), BF16),
            jax.ShapeDtypeStruct((slots, block, rank), BF16),
        ),
        in_specs=[smem, smem, VMEM, VMEM, HBM, HBM, HBM, HBM],
        out_specs=(VMEM, VMEM, VMEM, VMEM),
        scratch_shapes=[
            pltpu.VMEM((count, per_device, rank), BF16),
            pltpu.VMEM((tile, block, covar), BF16),
            pltpu.VMEM((tile, block, rank), BF16),
            pltpu.VMEM((tile, block, rank), BF16),
            pltpu.VMEM((slots, block, block), BF16),
            pltpu.VMEM((covar, rank), BF16),
            pltpu.VMEM((tile + 2, block, rank), F32),
            pltpu.VMEM((2, tile, rank), F32),
            pltpu.VMEM((2, tile, rank), F32),
            pltpu.VMEM((rank, covar), F32),
            pltpu.VMEM(lshape, F32),
            pltpu.VMEM((nr, 2, piece, rank), F32),
            pltpu.VMEM((nr, 2, piece, rank), F32),
            pltpu.VMEM((quad, piece, rank), F32),
            pltpu.VMEM((nc, piece, rank), F32),
            pltpu.SemaphoreType.DMA((7,)),
            pltpu.SemaphoreType.DMA((count,)),
            pltpu.SemaphoreType.DMA((count,)),
            pltpu.SemaphoreType.DMA((4,)),
            pltpu.SemaphoreType.DMA((4,)),
            pltpu.SemaphoreType.DMA((hops,)),
            pltpu.SemaphoreType.DMA((hops,)),
        ],
        compiler_params=pltpu.CompilerParams(
            collective_id=0, has_side_effects=True, vmem_limit_bytes=LIMIT_FIELD
        ),
    )(blocks, live, factors_v, link_beta, covariates, factors_u, noise_u, obs)


def add_kernel(day_blocks, step_link, blocks_ref, base_ref, grad_ref, term_ref, total_ref, beta_ref, nb_ref,
               next_ref, dv_ref, beta_out, acc_u, acc_v):
    acc_u[...] = base_ref[...]
    acc_v[...] = jnp.zeros_like(acc_v)
    wide = 4

    def turn(t, carry):
        for j in range(wide):
            slot = t * wide + j
            e = blocks_ref[0, slot]
            pb, db = e // day_blocks, lax.rem(e, day_blocks)
            acc_u[pb] += 0.5 * step_pixel * grad_ref[slot].astype(F32)
            acc_v[db] += term_ref[slot].astype(F32)
        return carry

    lax.fori_loop(0, grad_ref.shape[0] // wide, turn, 0)
    next_ref[...] = acc_u[...].astype(BF16)
    dv_ref[...] = acc_v[...].astype(BF16)
    old = beta_ref[...]
    beta_out[...] = old + 0.5 * step_link * (total_ref[...] - old) + math.sqrt(step_link) * nb_ref[...]


def run_add(day_blocks, step_link, blocks, base, grad, term, total, link_beta, noise_beta):
    tile, block, rank = base.shape
    return pl.pallas_call(
        functools.partial(add_kernel, day_blocks, step_link),
        out_shape=(
            jax.ShapeDtypeStruct((tile, block, rank), BF16),
            jax.ShapeDtypeStruct((day_blocks, block, rank), BF16),
            jax.ShapeDtypeStruct(link_beta.shape, F32),
        ),
        in_specs=[pl.BlockSpec(memory_space=pltpu.SMEM)] + [VMEM] * 6,
        out_specs=(VMEM, VMEM, VMEM),
        scratch_shapes=[
            pltpu.VMEM((tile, block, rank), F32),
            pltpu.VMEM((day_blocks, block, rank), F32),
        ],
        compiler_params=pltpu.CompilerParams(vmem_limit_bytes=LIMIT),
    )(blocks, base, grad, term, total, link_beta, noise_beta)


def sum_kernel(
    rows, cols, step_day, dv, fv_ref, nv_ref, v_ref,
    got_a, got_b, mid_a, mid_b, far_a, far_b, part_a, part_b, last_a, last_b, mid, got_z,
    send_sem, recv_sem,
):
    at = Place(rows, cols)
    nr, nc = at.nr, at.nc
    half = nc // 2
    greet(at.partners())
    used = [0]
    pending = []

    def post(src, dst, device):
        k = used[0]
        used[0] += 1
        copy = send(src, dst, send_sem.at[k], recv_sem.at[k], device)
        pending.append(copy)
        return copy

    def settle(copies):
        for copy in copies:
            copy.wait_recv()

    def summed(own, refs):
        part = own.astype(F32)
        for ref in refs:
            part = part + ref.astype(F32)
        return part

    first, second = pl.ds(0, half), pl.ds(half, half)
    a = [post(dv.at[:, 1 - at.r0, first], got_a, at.core)]
    b = [post(dv.at[:, 1 - at.r0, second], got_b, at.core)]
    settle(a)
    mid_a[...] = summed(dv[:, at.r0, first], [got_a[...]]).astype(BF16)
    a = [post(mid_a.at[at.r1_at(k)], far_a.at[k - 1], at.x_peer(k)) for k in range(1, nr)]
    settle(b)
    mid_b[...] = summed(dv[:, at.r0, second], [got_b[...]]).astype(BF16)
    b = [post(mid_b.at[:, :, 1 - at.c0], far_b, at.side)]
    settle(a)
    part_a[...] = summed(mid_a[at.r1], [far_a[k] for k in range(nr - 1)]).astype(BF16)
    a = [post(part_a.at[:, 1 - at.c0], last_a, at.side)]
    settle(b)
    part_b[...] = summed(mid_b[:, :, at.c0], [far_b[...]]).astype(BF16)
    b = [post(part_b.at[at.r1_at(k)], last_b.at[k - 1], at.x_peer(k)) for k in range(1, nr)]
    settle(a)
    mid[first] = summed(part_a[:, at.c0], [last_a[...]]).astype(BF16)
    settle(b)
    mid[second] = summed(part_b[at.r1], [last_b[k] for k in range(nr - 1)]).astype(BF16)
    a = [post(mid.at[at.c1_at(k)], got_z.at[k - 1], at.z_peer(k)) for k in range(1, nc)]
    settle(a)
    part = summed(mid[at.c1], [got_z[k] for k in range(nc - 1)])
    old = fv_ref[...]
    v_ref[...] = old + 0.5 * step_day * (part - old) + math.sqrt(step_day) * nv_ref[...]
    for copy in pending:
        copy.wait_send()


def run_sum(rows, cols, step_day, dv, factors_v, noise_v):
    nr, nc = rows // 2, cols // 2
    half = nc // 2
    per_device, rank = factors_v.shape
    sends = 2 * (1 + (nr - 1) + 1) + (nc - 1)
    buf = lambda *lead: pltpu.VMEM((*lead, per_device, rank), BF16)
    return pl.pallas_call(
        functools.partial(sum_kernel, rows, cols, step_day),
        out_shape=jax.ShapeDtypeStruct((per_device, rank), F32),
        in_specs=[VMEM] * 3,
        out_specs=VMEM,
        scratch_shapes=[
            buf(nr, half, 2), buf(nr, half, 2),
            buf(nr, half, 2), buf(nr, half, 2),
            buf(nr - 1, half, 2), buf(nr, half),
            buf(half, 2), buf(nr, half),
            buf(half), buf(nr - 1, half),
            buf(nc), buf(nc - 1),
            pltpu.SemaphoreType.DMA((sends,)),
            pltpu.SemaphoreType.DMA((sends,)),
        ],
        compiler_params=pltpu.CompilerParams(
            collective_id=1, has_side_effects=True, vmem_limit_bytes=LIMIT
        ),
    )(dv.reshape(nr, 2, nc, 2, per_device, rank), factors_v, noise_v)


def shards(
    factors_u, covariates, link_beta, factors_v, obs_values, obs_blocks, obs_count,
    noise_u, noise_v, noise_beta,
):
    rows = lax.axis_size("row")
    cols = lax.axis_size("col")
    devices = rows * cols
    tile, block, rank = factors_u.shape
    per_device = factors_v.shape[0]
    days = per_device * devices
    day_blocks = days // block
    slots = obs_blocks.shape[1]
    step_day = 0.25 / math.sqrt(devices * slots * block / day_blocks)
    step_link = 0.25 / math.sqrt(devices * tile * block)
    base, total, grad, term = run_field(
        rows, cols, obs_blocks, obs_count, factors_v, link_beta, covariates, factors_u, noise_u,
        obs_values[0],
    )
    u_next, dv, beta_next = run_add(
        day_blocks, step_link, obs_blocks, base, grad, term,
        total.reshape(link_beta.shape), link_beta, noise_beta,
    )
    v_next = run_sum(rows, cols, step_day, dv, factors_v, noise_v)
    return (u_next, v_next, beta_next)


def solution(mesh):
    in_specs = (
        P("row", "col", None),
        P("row", "col", None),
        P(),
        P(("row", "col"), None),
        P(("row", "col"), None, None, None),
        P(("row", "col"), None),
        P(("row", "col")),
        P("row", "col", None),
        P(("row", "col"), None),
        P(),
    )
    out_specs = (P("row", "col", None), P(("row", "col"), None), P())
    return jax.shard_map(shards, mesh=mesh, in_specs=in_specs, out_specs=out_specs, check_vma=False)
```

```python
import functools
import math

import jax
import jax.numpy as jnp
from jax import lax
from jax.experimental import pallas as pl
from jax.experimental.pallas import tpu as pltpu
from jax.sharding import PartitionSpec as P

edge_weight = 0.5
ridge_weight = 0.1
step_pixel = 0.2
MESH = pl.DeviceIdType.MESH
F32 = jnp.float32
BF16 = jnp.bfloat16
VMEM = pl.BlockSpec(memory_space=pltpu.VMEM)
HBM = pl.BlockSpec(memory_space=pltpu.HBM)
LIMIT = 40 * 1024 * 1024
LIMIT_FIELD = 40 * 1024 * 1024


class Place:
    def __init__(self, rows, cols):
        self.rows, self.cols = rows, cols
        self.nr, self.nc = rows // 2, cols // 2
        self.r, self.c = lax.axis_index("row"), lax.axis_index("col")
        self.r1, self.r0 = self.r // 2, lax.rem(self.r, 2)
        self.c1, self.c0 = self.c // 2, lax.rem(self.c, 2)
        self.core = (self.r1 * 2 + (1 - self.r0), self.c)
        self.side = (self.r, self.c1 * 2 + (1 - self.c0))

    def r1_at(self, k):
        return lax.rem(self.r1 + k, self.nr)

    def c1_at(self, k):
        return lax.rem(self.c1 + k, self.nc)

    def x_peer(self, k):
        return (self.r1_at(k) * 2 + self.r0, self.c)

    def z_peer(self, k):
        return (self.r, self.c1_at(k) * 2 + self.c0)

    def quad(self):
        found = []
        for k in range(self.nr):
            for c0 in (self.c0, 1 - self.c0):
                if k or c0 is not self.c0:
                    r1 = self.r1_at(k)
                    found.append(((r1 * 2 + self.r0, self.c1 * 2 + c0), r1, c0))
        return found

    def partners(self):
        return (
            [self.core, self.side]
            + [self.x_peer(k) for k in range(1, self.nr)]
            + [self.z_peer(k) for k in range(1, self.nc)]
        )


def greet(partners):
    barrier = pltpu.get_barrier_semaphore()
    for partner in partners:
        pl.semaphore_signal(barrier, inc=1, device_id=partner, device_id_type=MESH)
    pl.semaphore_wait(barrier, len(partners))


def send(src, dst, send_sem, recv_sem, device):
    copy = pltpu.make_async_remote_copy(
        src_ref=src, dst_ref=dst, send_sem=send_sem, recv_sem=recv_sem,
        device_id=device, device_id_type=MESH,
    )
    copy.start()
    return copy


def field_kernel(
    rows, cols, blocks_ref, live_ref, fv_ref, beta_ref, cov_hbm, u_hbm, obs_hbm,
    base_ref, total, grad_ref, term_ref,
    days, cov, u, obs, beta, rp, edge_send, edge_recv, link_acc,
    lk, lk_core, lm_core, lk_quad, lk_z,
    load_sem, day_send, day_recv, halo_send, halo_recv, link_send, link_recv,
):
    at = Place(rows, cols)
    nr, nc = at.nr, at.nc
    tile, block = u.shape[0], u.shape[1]
    parts = 4
    per = tile // parts
    loads = []
    for k in range(parts):
        loads.append(pltpu.make_async_copy(cov_hbm.at[pl.ds(k * per, per)], cov.at[pl.ds(k * per, per)], load_sem.at[k]))
    u_load = pltpu.make_async_copy(u_hbm, u, load_sem.at[parts])
    loads[0].start()
    u_load.start()
    for load in loads[1:]:
        load.start()
    obs_load = pltpu.make_async_copy(obs_hbm, obs, load_sem.at[parts + 1])
    obs_load.start()

    def index_of(b):
        return ((b[0] * 2 + b[1]) * nc + b[2]) * 2 + b[3]

    days[at.r * cols + at.c] = fv_ref[...].astype(BF16)
    north = (lax.rem(at.r + rows - 1, rows), at.c)
    south = (lax.rem(at.r + 1, rows), at.c)
    west = (at.r, lax.rem(at.c + cols - 1, cols))
    east = (at.r, lax.rem(at.c + 1, cols))
    quad = at.quad()
    greet(
        [at.core] + [q[0] for q in quad] + [at.z_peer(k) for k in range(1, nc)]
        + [north, south, west, east]
    )

    sends = []

    def block_at(b):
        return days.at[index_of(b)]

    def sem_at(b):
        return day_recv.at[index_of(b)]

    def pass_on(b, partners):
        for partner in partners:
            sends.append(send(block_at(b), block_at(b), day_send.at[len(sends)], sem_at(b), partner))

    def arrive(b):
        pltpu.make_async_remote_copy(
            src_ref=block_at(b), dst_ref=block_at(b), send_sem=day_send.at[0], recv_sem=sem_at(b),
            device_id=at.core, device_id_type=MESH,
        ).wait_recv()

    zs = [at.z_peer(k) for k in range(1, nc)]
    xs = [at.x_peer(k) for k in range(1, nr)]
    own = (at.r1, at.r0, at.c1, at.c0)
    pass_on(own, zs + [at.side] + xs + [at.core])

    beta[...] = beta_ref[...].astype(BF16)

    def resid_rows(i):
        cells = cov[pl.ds(i, per)].reshape(per * block, cov.shape[2])
        mean = jnp.dot(cells, beta[...], preferred_element_type=F32)
        rp[pl.ds(i + 1, per)] = u[pl.ds(i, per)].astype(F32) - mean.reshape(per, block, -1)

    u_load.wait()
    for k in range(parts):
        loads[k].wait()
        resid_rows(k * per)
    edge_send[0] = rp[pl.ds(1, tile), 0, :]
    edge_send[1] = rp[pl.ds(1, tile), block - 1, :]
    halos = [
        send(rp.at[1], rp.at[tile + 1], halo_send.at[0], halo_recv.at[0], north),
        send(rp.at[tile], rp.at[0], halo_send.at[1], halo_recv.at[1], south),
        send(edge_send.at[0], edge_recv.at[1], halo_send.at[2], halo_recv.at[2], west),
        send(edge_send.at[1], edge_recv.at[0], halo_send.at[3], halo_recv.at[3], east),
    ]

    for k in range(1, nc):
        b = (at.r1, at.r0, at.c1_at(nc - k), at.c0)
        arrive(b)
        pass_on(b, [at.side] + xs + [at.core])
    for k in range(nc):
        b = (at.r1, at.r0, at.c1_at(nc - k), 1 - at.c0)
        arrive(b)
        pass_on(b, (xs if k % 2 == 0 else []) + [at.core])

    for halo in halos:
        halo.wait()
    for spot, gone in ((0, at.r == 0), (tile + 1, at.r == rows - 1)):
        rp[spot] = jnp.where(gone, 0.0, rp[spot])
    for spot, gone in ((0, at.c == 0), (1, at.c == cols - 1)):
        edge_recv[spot] = jnp.where(gone, 0.0, edge_recv[spot])

    lane_row = lax.broadcasted_iota(jnp.int32, (per, block, u.shape[2]), 1)

    def prior_rows(i):
        mid = rp[pl.ds(i + 1, per)]
        around = rp[pl.ds(i, per)] + rp[pl.ds(i + 2, per)]
        left = jnp.where(lane_row == 0, edge_recv[0, pl.ds(i, per)][:, None, :], pltpu.roll(mid, 1, 1))
        right = jnp.where(
            lane_row == block - 1, edge_recv[1, pl.ds(i, per)][:, None, :], pltpu.roll(mid, block - 1, 1)
        )
        laplace = 4.0 * mid - (around + right + left)
        prior = edge_weight * laplace + ridge_weight * mid
        base_ref[pl.ds(i, per)] = (
            u[pl.ds(i, per)].astype(F32)
            - 0.5 * step_pixel * prior
        )
        return lax.dot_general(
            prior.astype(BF16).reshape(per * block, -1),
            cov[pl.ds(i, per)].reshape(per * block, cov.shape[2]),
            (((0,), (0,)), ((), ())),
            preferred_element_type=F32,
        )

    for k in range(parts):
        if k == 0:
            link_acc[...] = prior_rows(0)
        else:
            link_acc[...] += prior_rows(k * per)

    lk[...] = link_acc[...].T.reshape(lk.shape)
    used = [0]
    pending = []

    def post(src, dst, device):
        k = used[0]
        used[0] += 1
        copy = send(src, dst, link_send.at[k], link_recv.at[k], device)
        pending.append(copy)
        return copy

    def settle(copies):
        for copy in copies:
            copy.wait_recv()

    hop = [post(lk.at[1 - at.r0], lk_core, at.core)]
    for j in range(1, nr):
        for k in range(nc):
            b = (at.r1_at(nr - j), at.r0, at.c1_at(nc - k), at.c0)
            arrive(b)
            pass_on(b, ([at.side] if k % 2 else []) + [at.core])
    settle(hop)
    lm_core[...] = lk[at.r0] + lk_core[...]
    hop = [
        post(lm_core.at[r1, c0], lk_quad.at[q], device)
        for q, (device, r1, c0) in enumerate(quad)
    ]
    for j in range(1, nr):
        for k in range(nc):
            b = (at.r1_at(nr - j), at.r0, at.c1_at(nc - k), 1 - at.c0)
            arrive(b)
            pass_on(b, [at.core])
    for j in range(nr):
        for k in range(nc):
            for c0 in (at.c0, 1 - at.c0):
                arrive((at.r1_at(nr - j), 1 - at.r0, at.c1_at(nc - k), c0))
    obs_load.wait()

    live = live_ref[0]
    day_blocks = days.shape[0] * days.shape[1] // block
    span = block // days.shape[1]
    slots = obs.shape[0]
    wide = 16
    stages = 3
    turns = slots // wide

    def turn(t, carry):
        taken = []
        for j in range(wide):
            slot = t * wide + j
            e = blocks_ref[0, slot]
            pb, db = e // day_blocks, lax.rem(e, day_blocks)
            taken.append((slot, u[pb], days[pl.ds(db * span, span)].reshape(block, u.shape[2]), obs[slot]))
        resid = []
        for slot, uu, vv, yy in taken:
            predicted = lax.dot_general(uu, vv, (((1,), (1,)), ((), ())), preferred_element_type=F32)
            resid.append(jnp.where(slot < live, yy.astype(F32) - predicted, 0.0).astype(BF16))
        grads = [
            jnp.dot(res, vv, preferred_element_type=F32).astype(BF16)
            for res, (_, _, vv, _) in zip(resid, taken)
        ]
        terms = [
            lax.dot_general(res, uu, (((0,), (0,)), ((), ())), preferred_element_type=F32).astype(BF16)
            for res, (_, uu, _, _) in zip(resid, taken)
        ]
        for (slot, _, _, _), grad, term in zip(taken, grads, terms):
            grad_ref[slot] = grad
            term_ref[slot] = term
        return carry

    for stage in range(stages + 1):
        lax.fori_loop(stage * turns // (stages + 1), (stage + 1) * turns // (stages + 1), turn, 0)
        settle(hop)
        if stage == 0:
            link = lm_core[at.r1, at.c0]
            for q in range(len(quad)):
                link = link + lk_quad[q]
            lk_z[at.c1] = link
            hop = [post(lk_z.at[at.c1], lk_z.at[at.c1], at.z_peer(k)) for k in range(1, nc)]
        elif stage == 1:
            link = lk_z[0]
            for k in range(1, nc):
                link = link + lk_z[k]
            own_piece = total.at[at.r0, at.r1, at.c0]
            own_piece[...] = link
            hop = [post(own_piece, own_piece, device) for device, _, _ in quad]
        elif stage == 2:
            hop = [post(total.at[at.r0], total.at[at.r0], at.core)]
        else:
            hop = []
    for copy in sends + pending:
        copy.wait_send()


def run_field(rows, cols, blocks, live, factors_v, link_beta, covariates, factors_u, obs):
    tile, block, rank = factors_u.shape
    covar = covariates.shape[2]
    per_device = factors_v.shape[0]
    slots = obs.shape[0]
    count = rows * cols
    nr, nc = rows // 2, cols // 2
    piece = covar // (4 * nr)
    lshape = (2, nr, 2, piece, rank)
    quad = 2 * nr - 1
    hops = 2 * (1 + quad) + (nc - 1)
    smem = pl.BlockSpec(memory_space=pltpu.SMEM)
    return pl.pallas_call(
        functools.partial(field_kernel, rows, cols),
        out_shape=(
            jax.ShapeDtypeStruct((tile, block, rank), F32),
            jax.ShapeDtypeStruct(lshape, F32),
            jax.ShapeDtypeStruct((slots, block, rank), BF16),
            jax.ShapeDtypeStruct((slots, block, rank), BF16),
        ),
        in_specs=[smem, smem, VMEM, VMEM, HBM, HBM, HBM],
        out_specs=(VMEM, VMEM, VMEM, VMEM),
        scratch_shapes=[
            pltpu.VMEM((count, per_device, rank), BF16),
            pltpu.VMEM((tile, block, covar), BF16),
            pltpu.VMEM((tile, block, rank), BF16),
            pltpu.VMEM((slots, block, block), BF16),
            pltpu.VMEM((covar, rank), BF16),
            pltpu.VMEM((tile + 2, block, rank), F32),
            pltpu.VMEM((2, tile, rank), F32),
            pltpu.VMEM((2, tile, rank), F32),
            pltpu.VMEM((rank, covar), F32),
            pltpu.VMEM(lshape, F32),
            pltpu.VMEM((nr, 2, piece, rank), F32),
            pltpu.VMEM((nr, 2, piece, rank), F32),
            pltpu.VMEM((quad, piece, rank), F32),
            pltpu.VMEM((nc, piece, rank), F32),
            pltpu.SemaphoreType.DMA((6,)),
            pltpu.SemaphoreType.DMA((count,)),
            pltpu.SemaphoreType.DMA((count,)),
            pltpu.SemaphoreType.DMA((4,)),
            pltpu.SemaphoreType.DMA((4,)),
            pltpu.SemaphoreType.DMA((hops,)),
            pltpu.SemaphoreType.DMA((hops,)),
        ],
        compiler_params=pltpu.CompilerParams(
            collective_id=0, has_side_effects=True, vmem_limit_bytes=LIMIT_FIELD
        ),
    )(blocks, live, factors_v, link_beta, covariates, factors_u, obs)


def add_kernel(day_blocks, step_link, blocks_ref, base_ref, nz_ref, grad_ref, term_ref, total_ref, beta_ref, nb_ref,
               next_ref, dv_ref, beta_out, acc_u, acc_v):
    acc_u[...] = base_ref[...] + math.sqrt(step_pixel) * nz_ref[...].astype(F32)
    acc_v[...] = jnp.zeros_like(acc_v)
    wide = 4

    def turn(t, carry):
        for j in range(wide):
            slot = t * wide + j
            e = blocks_ref[0, slot]
            pb, db = e // day_blocks, lax.rem(e, day_blocks)
            acc_u[pb] += 0.5 * step_pixel * grad_ref[slot].astype(F32)
            acc_v[db] += term_ref[slot].astype(F32)
        return carry

    lax.fori_loop(0, grad_ref.shape[0] // wide, turn, 0)
    next_ref[...] = acc_u[...].astype(BF16)
    dv_ref[...] = acc_v[...].astype(BF16)
    old = beta_ref[...]
    beta_out[...] = old + 0.5 * step_link * (total_ref[...] - old) + math.sqrt(step_link) * nb_ref[...]


def run_add(day_blocks, step_link, blocks, base, noise_u, grad, term, total, link_beta, noise_beta):
    tile, block, rank = base.shape
    return pl.pallas_call(
        functools.partial(add_kernel, day_blocks, step_link),
        out_shape=(
            jax.ShapeDtypeStruct((tile, block, rank), BF16),
            jax.ShapeDtypeStruct((day_blocks, block, rank), BF16),
            jax.ShapeDtypeStruct(link_beta.shape, F32),
        ),
        in_specs=[pl.BlockSpec(memory_space=pltpu.SMEM)] + [VMEM] * 7,
        out_specs=(VMEM, VMEM, VMEM),
        scratch_shapes=[
            pltpu.VMEM((tile, block, rank), F32),
            pltpu.VMEM((day_blocks, block, rank), F32),
        ],
        compiler_params=pltpu.CompilerParams(vmem_limit_bytes=LIMIT),
    )(blocks, base, noise_u, grad, term, total, link_beta, noise_beta)


def sum_kernel(
    rows, cols, step_day, dv, fv_ref, nv_ref, v_ref,
    got_a, got_b, mid_a, mid_b, far_a, far_b, part_a, part_b, last_a, last_b, mid, got_z,
    send_sem, recv_sem,
):
    at = Place(rows, cols)
    nr, nc = at.nr, at.nc
    half = nc // 2
    greet(at.partners())
    used = [0]
    pending = []

    def post(src, dst, device):
        k = used[0]
        used[0] += 1
        copy = send(src, dst, send_sem.at[k], recv_sem.at[k], device)
        pending.append(copy)
        return copy

    def settle(copies):
        for copy in copies:
            copy.wait_recv()

    def summed(own, refs):
        part = own.astype(F32)
        for ref in refs:
            part = part + ref.astype(F32)
        return part

    first, second = pl.ds(0, half), pl.ds(half, half)
    a = [post(dv.at[:, 1 - at.r0, first], got_a, at.core)]
    b = [post(dv.at[:, 1 - at.r0, second], got_b, at.core)]
    settle(a)
    mid_a[...] = summed(dv[:, at.r0, first], [got_a[...]]).astype(BF16)
    a = [post(mid_a.at[at.r1_at(k)], far_a.at[k - 1], at.x_peer(k)) for k in range(1, nr)]
    settle(b)
    mid_b[...] = summed(dv[:, at.r0, second], [got_b[...]]).astype(BF16)
    b = [post(mid_b.at[:, :, 1 - at.c0], far_b, at.side)]
    settle(a)
    part_a[...] = summed(mid_a[at.r1], [far_a[k] for k in range(nr - 1)]).astype(BF16)
    a = [post(part_a.at[:, 1 - at.c0], last_a, at.side)]
    settle(b)
    part_b[...] = summed(mid_b[:, :, at.c0], [far_b[...]]).astype(BF16)
    b = [post(part_b.at[at.r1_at(k)], last_b.at[k - 1], at.x_peer(k)) for k in range(1, nr)]
    settle(a)
    mid[first] = summed(part_a[:, at.c0], [last_a[...]]).astype(BF16)
    settle(b)
    mid[second] = summed(part_b[at.r1], [last_b[k] for k in range(nr - 1)]).astype(BF16)
    a = [post(mid.at[at.c1_at(k)], got_z.at[k - 1], at.z_peer(k)) for k in range(1, nc)]
    settle(a)
    part = summed(mid[at.c1], [got_z[k] for k in range(nc - 1)])
    old = fv_ref[...]
    v_ref[...] = old + 0.5 * step_day * (part - old) + math.sqrt(step_day) * nv_ref[...]
    for copy in pending:
        copy.wait_send()


def run_sum(rows, cols, step_day, dv, factors_v, noise_v):
    nr, nc = rows // 2, cols // 2
    half = nc // 2
    per_device, rank = factors_v.shape
    sends = 2 * (1 + (nr - 1) + 1) + (nc - 1)
    buf = lambda *lead: pltpu.VMEM((*lead, per_device, rank), BF16)
    return pl.pallas_call(
        functools.partial(sum_kernel, rows, cols, step_day),
        out_shape=jax.ShapeDtypeStruct((per_device, rank), F32),
        in_specs=[VMEM] * 3,
        out_specs=VMEM,
        scratch_shapes=[
            buf(nr, half, 2), buf(nr, half, 2),
            buf(nr, half, 2), buf(nr, half, 2),
            buf(nr - 1, half, 2), buf(nr, half),
            buf(half, 2), buf(nr, half),
            buf(half), buf(nr - 1, half),
            buf(nc), buf(nc - 1),
            pltpu.SemaphoreType.DMA((sends,)),
            pltpu.SemaphoreType.DMA((sends,)),
        ],
        compiler_params=pltpu.CompilerParams(
            collective_id=1, has_side_effects=True, vmem_limit_bytes=LIMIT
        ),
    )(dv.reshape(nr, 2, nc, 2, per_device, rank), factors_v, noise_v)


def shards(
    factors_u, covariates, link_beta, factors_v, obs_values, obs_blocks, obs_count,
    noise_u, noise_v, noise_beta,
):
    rows = lax.axis_size("row")
    cols = lax.axis_size("col")
    devices = rows * cols
    tile, block, rank = factors_u.shape
    per_device = factors_v.shape[0]
    days = per_device * devices
    day_blocks = days // block
    slots = obs_blocks.shape[1]
    step_day = 0.25 / math.sqrt(devices * slots * block / day_blocks)
    step_link = 0.25 / math.sqrt(devices * tile * block)
    base, total, grad, term = run_field(
        rows, cols, obs_blocks, obs_count, factors_v, link_beta, covariates, factors_u, obs_values[0],
    )
    u_next, dv, beta_next = run_add(
        day_blocks, step_link, obs_blocks, base, noise_u, grad, term,
        total.reshape(link_beta.shape), link_beta, noise_beta,
    )
    v_next = run_sum(rows, cols, step_day, dv, factors_v, noise_v)
    return (u_next, v_next, beta_next)


def solution(mesh):
    in_specs = (
        P("row", "col", None),
        P("row", "col", None),
        P(),
        P(("row", "col"), None),
        P(("row", "col"), None, None, None),
        P(("row", "col"), None),
        P(("row", "col")),
        P("row", "col", None),
        P(("row", "col"), None),
        P(),
    )
    out_specs = (P("row", "col", None), P(("row", "col"), None), P())
    return jax.shard_map(shards, mesh=mesh, in_specs=in_specs, out_specs=out_specs, check_vma=False)
```
